256 devices in a mesh: dp: 64 (over x, z, core), tensor: 4 (over y).
Axes of the slice: x: 4, y: 4, z: 8, core: 2. Of those that a mesh axis runs over, the one named last changes fastest.
Arguments:
- gradient: bfloat16 [8, 5120, 13824], P(None, 'dp', 'tensor'), may hold values from -16 to 16
- error_buffer: bfloat16 [8, 5120, 13824], P(None, 'dp', 'tensor'), may hold values from -6 to 6
- q_start: bfloat16 [13824, 64], P('tensor'), may hold values from -6 to 6
Outputs:
- new_error: bfloat16 [8, 5120, 13824], P(None, 'dp', 'tensor')
- q_factor: float32 [13824, 64], P('tensor')
The draws below stay inside these ranges and needn't reach their ends.
All inputs are finite; a program needn't handle non-finite values.
Results may differ from the reference program's by a relative error of at most 0.015.
Values may be sent and summed in bfloat16 or wider, within the bound.
No kernel may reach another device: no remote copies, remote signals or barrier semaphores. Data moves between devices by JAX's collectives and lax.ppermute only.
A program may use at most 64 MiB of HBM per device.

```python
import jax
import jax.numpy as jnp
from jax import lax

D = 5120
FF = 13824
RANK = 64
ITERS = 2
REPL = 8


def draw_gradient(key, part):
    key = jax.random.fold_in(key, 11)
    key_noise = jax.random.fold_in(key, 0)
    key_rows = jax.random.fold_in(key, 1)
    key_cols = jax.random.fold_in(key, 2)
    key_left = jax.random.fold_in(key, 4)
    key_right = jax.random.fold_in(key, 5)
    rise = 3.0 ** (jnp.arange(D, dtype=jnp.float32) / D)
    row_factor = rise * jnp.exp(jax.random.uniform(key_rows, (D,), jnp.float32, 0.0, 1.3862944))
    col_factor = jnp.exp(jax.random.uniform(key_cols, (FF,), jnp.float32, 0.0, 1.3862944))
    scale = row_factor[:, None] * col_factor[None, :] * 0.25
    weights = 10.0 ** (-jnp.arange(RANK, dtype=jnp.float32) / (RANK - 1))
    left = jax.random.normal(key_left, (D, RANK), jnp.float32) * weights[None, :]
    right = jax.random.normal(key_right, (FF, RANK), jnp.float32)
    lowrank = jnp.dot(left, right.T, precision=lax.Precision.HIGHEST) / jnp.sqrt(jnp.sum(weights * weights))
    base = jax.random.normal(key_noise, (REPL, D, FF), jnp.float32) + 0.35 * lowrank[None]
    return jnp.clip(base * scale[None], -16.0, 16.0).astype(jnp.bfloat16)


def levels(stream_key, shape, cuts, low, largest):
    level = 1.0
    for axis_at, parts in cuts:
        heights = jax.random.uniform(jax.random.fold_in(jax.random.fold_in(stream_key, 6), axis_at), (parts,), jnp.float32, low / len(cuts), largest / len(cuts))
        level = level * jnp.repeat(jnp.exp(heights), shape[axis_at] // parts).reshape((-1,) + (1,) * (len(shape) - 1 - axis_at))
    return level


def bell_draw(own_key, extent, scale, bound, cuts=(), kind=jnp.bfloat16):
    factor_of = levels(own_key, extent, cuts, -0.22, 0.18) if cuts else 1.0
    entries = jax.random.normal(own_key, extent, jnp.float32) * scale * factor_of
    return jnp.minimum(jnp.maximum(entries, -bound), bound).astype(kind)


def setup_inputs(seed: int = 0) -> dict:
    seeds = jax.random.split(jax.random.key(seed), 4)
    return {
        "gradient": draw_gradient(jax.random.fold_in(seeds[3], 71), 0),
        "error_buffer": bell_draw(seeds[1], (REPL, D, FF), 0.5, 6.0, ((1, 64), (2, 4))),
        "q_start": bell_draw(seeds[2], (FF, RANK), 1.0, 6.0, ((0, 4),)),
    }


def orthonormal(p_mean):
    gram = jnp.dot(p_mean.T, p_mean, precision=lax.Precision.HIGHEST)
    lower = jnp.linalg.cholesky(gram)
    return jax.scipy.linalg.solve_triangular(lower, p_mean.T, lower=True).T

def reference(gradient, error_buffer, q_start):
    corrected = [(gradient[index].astype(jnp.float32) + error_buffer[index].astype(jnp.float32)).astype(jnp.bfloat16) for index in range(REPL)]
    q_half = q_start
    q_now = None
    p_half = None
    for step in range(ITERS):
        p_sum = jnp.zeros((D, RANK), jnp.float32)
        for index in range(REPL):
            p_sum = p_sum + jnp.dot(corrected[index].astype(jnp.float32), q_half.astype(jnp.float32), preferred_element_type=jnp.float32)
        p_half = orthonormal(p_sum / REPL).astype(jnp.bfloat16)
        q_sum = jnp.zeros((FF, RANK), jnp.float32)
        for index in range(REPL):
            q_sum = q_sum + jnp.dot(corrected[index].T.astype(jnp.float32), p_half.astype(jnp.float32), preferred_element_type=jnp.float32)
        q_now = q_sum / REPL
        q_half = q_now.astype(jnp.bfloat16)
    recon = jnp.dot(p_half.astype(jnp.float32), q_half.T.astype(jnp.float32), preferred_element_type=jnp.float32)
    new_error = jnp.stack([(corrected[index].astype(jnp.float32) - recon).astype(jnp.bfloat16) for index in range(REPL)])
    return (new_error, q_now)
```

```python
import functools

import jax
import jax.numpy as jnp
from jax import lax
from jax.experimental import pallas as pl
from jax.experimental.pallas import tpu as pltpu
from jax.sharding import Mesh
from jax.sharding import PartitionSpec as P

X, Z, CORES, Y = 4, 8, 2, 4
PEERS = X * Z
LANES = 128
F32, BF16 = jnp.float32, jnp.bfloat16
HIGH = lax.Precision.HIGHEST
VMEM = pl.BlockSpec(memory_space=pltpu.VMEM)
SMEM = pl.BlockSpec(memory_space=pltpu.SMEM)


def split(value):
    high = value.astype(BF16)
    return high, (value - high.astype(F32)).astype(BF16)


def dot(a, b, contract=((1,), (0,)), precision=None):
    return lax.dot_general(a, b, (contract, ((), ())), precision=precision, preferred_element_type=F32)


def params(mib, **more):
    return pltpu.CompilerParams(vmem_limit_bytes=mib << 20, **more)


def start_kernel(g_ref, e_ref, q_ref, corrected_ref, high_ref, low_ref, p_ref):
    replicas = g_ref.shape[0]
    total = jnp.zeros(g_ref.shape[1:], F32)
    for index in range(replicas):
        corrected = (g_ref[index].astype(F32) + e_ref[index].astype(F32)).astype(BF16)
        corrected_ref[index] = corrected
        total = total + corrected.astype(F32)
    high, low = split(total * (1.0 / replicas))
    high_ref[...] = high
    low_ref[...] = low
    term = dot(high, q_ref[...]) + dot(low, q_ref[...])

    @pl.when(pl.program_id(0) == 0)
    def _():
        p_ref[...] = term

    @pl.when(pl.program_id(0) > 0)
    def _():
        p_ref[...] += term


def start(gradient, error, q_start, width=384):
    replicas, rows, columns = gradient.shape
    rank = q_start.shape[1]
    wide = pl.BlockSpec((replicas, rows, width), lambda j: (0, 0, j))
    flat = pl.BlockSpec((rows, width), lambda j: (0, j))
    return pl.pallas_call(
        start_kernel,
        grid=(columns // width,),
        in_specs=[wide, wide, pl.BlockSpec((width, rank), lambda j: (j, 0))],
        out_specs=[wide, flat, flat, pl.BlockSpec((rows, rank), lambda j: (0, 0))],
        out_shape=[
            jax.ShapeDtypeStruct(gradient.shape, BF16),
            jax.ShapeDtypeStruct((rows, columns), BF16),
            jax.ShapeDtypeStruct((rows, columns), BF16),
            jax.ShapeDtypeStruct((rows, rank), F32),
        ],
        compiler_params=params(24),
    )(gradient, error, q_start)


def right_kernel(blocks, normed, core_ref, *refs):
    if normed:
        inverse_ref, *refs = refs
    own, one, two, three, high_ref, low_ref, mine_ref, theirs_ref, p_ref = refs
    p = (own[...] + two[...]) + (one[...] + three[...])
    if normed:
        p = dot(p, inverse_ref[...], ((1,), (1,)), HIGH)
    p_ref[...] = p
    rank = p.shape[1]
    half = rank // 2
    first = core_ref[0] == 0
    turned = p.T
    p_high, p_low = split(turned)
    both = jnp.concatenate([p_high, p_low], axis=0)
    for block in range(blocks):
        at = pl.ds(block * LANES, LANES)
        wide = dot(both, high_ref[:, at])
        u = wide[:rank] + (wide[rank:] + dot(p_high, low_ref[:, at]))
        mine_ref[block] = jnp.where(first, u[:half], u[half:])
        theirs_ref[block] = jnp.where(first, u[half:], u[:half])
    gram = dot(turned, p, ((1,), (0,)), HIGH)
    gram = jnp.concatenate([gram, jnp.zeros((rank, LANES - rank), F32)], axis=1)
    mine_ref[blocks] = jnp.where(first, gram[:half], gram[half:])
    theirs_ref[blocks] = jnp.where(first, gram[half:], gram[:half])


def right(core, parts, high, low, inverse=None):
    rows, columns = high.shape
    rank = parts[0].shape[1]
    blocks = columns // LANES
    shape = jax.ShapeDtypeStruct((blocks + 1, rank // 2, LANES), F32)
    operands = ([] if inverse is None else [inverse]) + list(parts) + [high, low]
    return pl.pallas_call(
        functools.partial(right_kernel, blocks, inverse is not None),
        in_specs=[SMEM] + [VMEM] * len(operands),
        out_specs=[VMEM] * 3,
        out_shape=[shape, shape, jax.ShapeDtypeStruct((rows, rank), F32)],
        compiler_params=params(24),
    )(core, *operands)


def add_kernel(a_ref, b_ref, out_ref):
    blocks = a_ref.shape[0]
    out_ref[:blocks] = a_ref[...] + b_ref[...]
    out_ref[blocks:] = jnp.zeros((out_ref.shape[0] - blocks,) + out_ref.shape[1:], F32)


def sum_kernel(in_ref, out_ref):
    total = in_ref[0]
    for peer in range(1, in_ref.shape[0]):
        total = total + in_ref[peer]
    for peer in range(out_ref.shape[0]):
        out_ref[peer] = total


def all_sum(mine, theirs):
    arrived = lax.ppermute(theirs, "core", [(0, 1), (1, 0)])
    shape = jax.ShapeDtypeStruct((PEERS,) + mine.shape[1:], F32)
    terms = pl.pallas_call(
        add_kernel, in_specs=[VMEM] * 2, out_specs=VMEM, out_shape=shape, compiler_params=params(8)
    )(mine, arrived)
    terms = lax.all_to_all(terms, ("x", "z"), 0, 0)
    sums = pl.pallas_call(
        sum_kernel, in_specs=[VMEM], out_specs=VMEM, out_shape=shape, compiler_params=params(8)
    )(terms)
    here = lax.all_to_all(sums, ("x", "z"), 0, 0)
    return here, lax.ppermute(here, "core", [(0, 1), (1, 0)])


def whole(first, a, b):
    return jnp.concatenate([jnp.where(first, a, b), jnp.where(first, b, a)], axis=0)


def left_kernel(core_ref, a_ref, b_ref, high_ref, low_ref, t_ref, gram_ref, u_ref):
    rank = gram_ref.shape[0]
    blocks = high_ref.shape[1] // LANES
    first = core_ref[0] == 0
    gram_ref[...] = whole(first, a_ref[blocks], b_ref[blocks])[:, :rank]
    for block in range(blocks):
        u_high, u_low = split(whole(first, a_ref[block], b_ref[block]))
        u_ref[:, pl.ds(block * LANES, LANES)] = jnp.concatenate([u_high, u_low], axis=0)
    wide = dot(high_ref[...], u_ref[...], ((1,), (1,)))
    t_ref[...] = wide[:, :rank] + (wide[:, rank:] + dot(low_ref[...], u_ref[:rank], ((1,), (1,))))


def left(core, a, b, high, low):
    rows, columns = high.shape
    rank = 2 * a.shape[1]
    return pl.pallas_call(
        left_kernel,
        in_specs=[SMEM] + [VMEM] * 4,
        out_specs=[VMEM] * 2,
        out_shape=[jax.ShapeDtypeStruct((rows, rank), F32), jax.ShapeDtypeStruct((rank, rank), F32)],
        scratch_shapes=[pltpu.VMEM((2 * rank, columns), BF16)],
        compiler_params=params(24),
    )(core, a, b, high, low)


def lower_inverse(gram):
    rank = gram.shape[0]
    at_row = lax.broadcasted_iota(jnp.int32, (rank, rank), 0)
    at_col = lax.broadcasted_iota(jnp.int32, (rank, rank), 1)
    work = jnp.concatenate([gram, (at_row == at_col).astype(F32)], axis=1)
    done = []
    for step in range(rank):
        low = step // 8 * 8
        here = work[low:]
        column = jnp.broadcast_to(here[:, step : step + 1], here.shape)
        at = step - low
        pivot = column[at : at + 1]
        row = here[at : at + 1]
        scale = lax.rsqrt(pivot)
        done.append((row * scale)[:, rank:])
        work = work[low:] - column * (row * (scale * scale)) if low == 0 else jnp.concatenate(
            [work[:low], here - column * (row * (scale * scale))], axis=0
        )
    return jnp.concatenate(done, axis=0)


def inverse_kernel(gram_ref, out_ref):
    out_ref[...] = lower_inverse(gram_ref[...])


def inverse_of(gram):
    return pl.pallas_call(
        inverse_kernel,
        in_specs=[VMEM],
        out_specs=VMEM,
        out_shape=jax.ShapeDtypeStruct(gram.shape, F32),
        compiler_params=params(4),
        cost_estimate=pl.CostEstimate(flops=10_000_000, bytes_accessed=5_000_000, transcendentals=0),
    )(gram)


def end_kernel(core_ref, a_ref, b_ref, p_ref, corrected_ref, new_ref, q_ref, inverse_ref, half_ref):
    rank = p_ref.shape[1]
    first = core_ref[0] == 0
    per = corrected_ref.shape[2] // LANES
    step = pl.program_id(0)
    last = pl.num_programs(0) * per

    @pl.when(step == 0)
    def _():
        inverse_ref[...] = lower_inverse(whole(first, a_ref[last], b_ref[last])[:, :rank])
        half_ref[...] = dot(p_ref[...], inverse_ref[...], ((1,), (1,)), HIGH).astype(BF16)

    for index in range(per):
        block = step * per + index
        u = whole(first, a_ref[block], b_ref[block])
        q = dot(inverse_ref[...], u, ((1,), (0,)), HIGH)
        q_ref[pl.ds(index * LANES, LANES), :] = q.T
        recon = dot(half_ref[...], q.astype(BF16))
        at = pl.ds(index * LANES, LANES)
        for replica in range(corrected_ref.shape[0]):
            new_ref[replica, :, at] = (corrected_ref[replica, :, at].astype(F32) - recon).astype(BF16)


def end(core, a, b, p, corrected, width=384):
    replicas, rows, columns = corrected.shape
    rank = p.shape[1]
    wide = pl.BlockSpec((replicas, rows, width), lambda j: (0, 0, j))
    return pl.pallas_call(
        end_kernel,
        grid=(columns // width,),
        in_specs=[SMEM, VMEM, VMEM, VMEM, wide],
        out_specs=[wide, pl.BlockSpec((width, rank), lambda j: (j, 0))],
        out_shape=[
            jax.ShapeDtypeStruct(corrected.shape, BF16),
            jax.ShapeDtypeStruct((columns, rank), F32),
        ],
        scratch_shapes=[pltpu.VMEM((rank, rank), F32), pltpu.VMEM((rows, rank), BF16)],
        compiler_params=params(24),
    )(core, a, b, p, corrected)


def around(value):
    return [value] + [lax.ppermute(value, "y", [(i, (i + k) % Y) for i in range(Y)]) for k in range(1, Y)]


def per_device(gradient, error_buffer, q_start):
    core = lax.axis_index("core").astype(jnp.int32).reshape(1)
    corrected, high, low, term = start(gradient, error_buffer, q_start)
    mine, theirs, _ = right(core, around(term), high, low)
    a, b = all_sum(mine, theirs)
    term, gram = left(core, a, b, high, low)
    parts = around(term)
    mine, theirs, p = right(core, parts, high, low, inverse_of(gram))
    a, b = all_sum(mine, theirs)
    return tuple(end(core, a, b, p, corrected))


def solution(mesh):
    fine = Mesh(mesh.devices.reshape(X, Z, CORES, Y), ("x", "z", "core", "y"))
    rows = ("x", "z", "core")
    return jax.shard_map(
        per_device,
        mesh=fine,
        in_specs=(P(None, rows, "y"), P(None, rows, "y"), P("y", None)),
        out_specs=(P(None, rows, "y"), P("y", None)),
        check_vma=False,
    )
```

```python
import functools

import jax
import jax.numpy as jnp
from jax import lax
from jax.experimental import pallas as pl
from jax.experimental.pallas import tpu as pltpu
from jax.sharding import Mesh
from jax.sharding import PartitionSpec as P

X, FAR, NEAR, CORES, Y = 4, 4, 2, 2, 4
LANES = 128
F32, BF16 = jnp.float32, jnp.bfloat16
HIGH = lax.Precision.HIGHEST
VMEM = pl.BlockSpec(memory_space=pltpu.VMEM)
SMEM = pl.BlockSpec(memory_space=pltpu.SMEM)


def split(value, parts):
    found = []
    for _ in range(parts):
        found.append(value.astype(BF16))
        value = value - found[-1].astype(F32)
    return found


def dot(a, b, contract=((1,), (0,)), precision=None):
    return lax.dot_general(a, b, (contract, ((), ())), precision=precision, preferred_element_type=F32)


def params(mib, **more):
    return pltpu.CompilerParams(vmem_limit_bytes=mib << 20, **more)


def start_kernel(height, g_ref, e_ref, q_ref, high_ref, low_ref, p_ref, g_near, e_near, q_near, sems, q_sem):
    replicas, rows, columns = g_ref.shape
    steps = rows // height
    copies = []
    for index in range(steps):
        at = (slice(None), pl.ds(index * height, height))
        copies.append([
            pltpu.make_async_copy(far.at[at], near.at[at], sems.at[which, index])
            for which, (far, near) in enumerate([(g_ref, g_near), (e_ref, e_near)])
        ])
        for copy in copies[-1]:
            copy.start()
        if index == 0:
            q_copy = pltpu.make_async_copy(q_ref, q_near, q_sem)
            q_copy.start()
    for index, pair in enumerate(copies):
        for copy in pair:
            copy.wait()
        row = pl.ds(index * height, height)
        for block in range(columns // LANES):
            at = pl.ds(block * LANES, LANES)
            total = (g_near[0, row, at] + e_near[0, row, at]).astype(F32)
            for replica in range(1, replicas):
                total = total + (g_near[replica, row, at] + e_near[replica, row, at]).astype(F32)
            high_ref[row, at], low_ref[row, at] = split(total * (1.0 / replicas), 2)
        if index >= steps - 2:
            if index == steps - 2:
                q_copy.wait()
                row = pl.ds(0, rows - height)
            both = jnp.concatenate([high_ref[row], low_ref[row]], axis=0)
            term = dot(both, q_near[...], ((1,), (1,)))
            p_ref[row] = term[: row.size] + term[row.size :]


def in_hbm(*values):
    return [pltpu.with_memory_space_constraint(value, pltpu.HBM) for value in values]


def start(gradient, error, q_turned, height=16):
    replicas, rows, columns = gradient.shape
    far = pl.BlockSpec(memory_space=pltpu.HBM)
    return pl.pallas_call(
        functools.partial(start_kernel, height),
        in_specs=[far] * 3,
        out_specs=[VMEM] * 3,
        out_shape=[
            jax.ShapeDtypeStruct((rows, columns), BF16),
            jax.ShapeDtypeStruct((rows, columns), BF16),
            jax.ShapeDtypeStruct((rows, q_turned.shape[0]), F32),
        ],
        scratch_shapes=[
            pltpu.VMEM(gradient.shape, BF16),
            pltpu.VMEM(error.shape, BF16),
            pltpu.VMEM(q_turned.shape, BF16),
            pltpu.SemaphoreType.DMA((2, rows // height)),
            pltpu.SemaphoreType.DMA,
        ],
        compiler_params=params(24),
    )(*in_hbm(gradient, error, q_turned))


def right_kernel(blocks, normed, core_ref, *refs):
    if normed:
        inverse_ref, *refs = refs
    own, one, two, three, high_ref, low_ref, mine_ref, theirs_ref, p_ref = refs
    p = (own[...] + two[...]) + (one[...] + three[...])
    if normed:
        p = dot(p, inverse_ref[...], ((1,), (1,)), HIGH)
    p_ref[...] = p
    rank = p.shape[1]
    half = rank // 2
    first = core_ref[0] == 0
    turned = p.T
    stack = jnp.concatenate(split(turned, 3), axis=0)
    for block in range(blocks):
        at = pl.ds(block * LANES, LANES)
        top = dot(stack, high_ref[:, at])
        low = dot(stack[: 2 * rank], low_ref[:, at])
        u = top[:rank] + ((top[rank : 2 * rank] + low[:rank]) + (top[2 * rank :] + low[rank:]))
        mine_ref[block] = jnp.where(first, u[:half], u[half:])
        theirs_ref[block] = jnp.where(first, u[half:], u[:half]).astype(theirs_ref.dtype)
    gram = dot(turned, p, ((1,), (0,)), HIGH)
    gram = jnp.concatenate([gram[:half], gram[half:]], axis=1)
    mine_ref[blocks] = gram
    if theirs_ref.dtype == F32:
        theirs_ref[blocks] = gram
    else:
        for index, part in enumerate(split(gram, 3)):
            theirs_ref[blocks + index] = part


def right(core, parts, high, low, inverse=None, kind=F32):
    rows, columns = high.shape
    rank = parts[0].shape[1]
    blocks = columns // LANES
    mine = jax.ShapeDtypeStruct((blocks + 1, rank // 2, LANES), F32)
    theirs = mine if kind == F32 else jax.ShapeDtypeStruct((blocks + 3, rank // 2, LANES), kind)
    operands = ([] if inverse is None else [inverse]) + list(parts) + [high, low]
    return pl.pallas_call(
        functools.partial(right_kernel, blocks, inverse is not None),
        in_specs=[SMEM] + [VMEM] * len(operands),
        out_specs=[VMEM] * 3,
        out_shape=[mine, theirs, jax.ShapeDtypeStruct((rows, rank), F32)],
        compiler_params=params(24),
    )(core, *operands)


def cut_kernel(x_ref, a_ref, b_ref, *out_refs):
    last = a_ref.shape[0] - 1
    per = out_refs[0].shape[0] - 1
    gram = a_ref[last] + b_ref[last]
    for flip, out_ref in enumerate(out_refs):
        at = pl.ds((x_ref[0] ^ flip) * per, per)
        out_ref[:per] = a_ref[at] + b_ref[at]
        out_ref[per] = gram


def four(refs, *at):
    own, one, two, three = [ref[at] if at else ref[...] for ref in refs]
    return (own + two) + (one + three)


def halve_kernel(near_ref, *refs):
    *in_refs, keep_ref, give_ref = refs
    rows = keep_ref.shape[1]
    place = near_ref[0] * rows
    keep_ref[...] = four(in_refs, slice(None), pl.ds(pl.multiple_of(place, rows), rows))
    give_ref[...] = four(in_refs, slice(None), pl.ds(pl.multiple_of(rows - place, rows), rows))


def two_kernel(a_ref, b_ref, out_ref):
    out_ref[...] = a_ref[...] + b_ref[...]


def four_kernel(*refs):
    refs[-1][...] = four(refs[:-1])


def join_kernel(near_ref, here_ref, there_ref, chunk_ref, gram_ref):
    per, rows = chunk_ref.shape[0], here_ref.shape[1]
    place = near_ref[0] * rows
    chunk_ref[:, pl.ds(pl.multiple_of(place, rows), rows)] = here_ref[:per]
    chunk_ref[:, pl.ds(pl.multiple_of(rows - place, rows), rows)] = there_ref[:per]
    first = near_ref[0] == 0
    here, there = here_ref[per], there_ref[per]
    packed = jnp.concatenate([jnp.where(first, here, there), jnp.where(first, there, here)], axis=0)
    half, rank = packed.shape[0], gram_ref.shape[0]
    gram_ref[:half] = packed[:, :rank]
    gram_ref[half:] = packed[:, rank:]


def small(kernel, operands, shapes, scalars=0, kind=F32, scratch=()):
    return pl.pallas_call(
        kernel,
        in_specs=[SMEM] * scalars + [VMEM] * (len(operands) - scalars),
        out_specs=[VMEM] * len(shapes),
        out_shape=[jax.ShapeDtypeStruct(shape, kind) for shape in shapes],
        scratch_shapes=scratch,
        compiler_params=params(8),
    )(*operands)


def pack(ref, u, gram):
    per = u.shape[0]
    ref[:per] = u.astype(BF16)
    parts = [part.astype(F32) for part in split(gram, 3)]
    spare = ref.shape[1] - 3 * gram.shape[0]
    ref[per] = jnp.concatenate(parts + [jnp.zeros((spare, LANES), F32)], axis=0).astype(BF16)


def unpack(ref):
    per, rows, _ = ref.shape
    block = ref[per - 1].astype(F32)
    part = rows // X
    return ref[: per - 1].astype(F32), block[:part] + (block[part : 2 * part] + block[2 * part : 3 * part])


def cut_coarse_kernel(x_ref, a_ref, b_ref, *refs):
    *out_refs, gram_ref = refs
    last = a_ref.shape[0] - 1
    per = out_refs[0].shape[0] - 1
    part = gram_ref.shape[0] // X
    gram = b_ref[last].astype(F32) + (b_ref[last + 1].astype(F32) + b_ref[last + 2].astype(F32))
    gram_ref[...] = a_ref[last] + gram
    for flip, out_ref in enumerate(out_refs):
        owner = x_ref[0] ^ flip
        at = pl.ds(owner * per, per)
        rows = pl.ds(pl.multiple_of(owner * part, part), part)
        pack(out_ref, a_ref[at] + b_ref[at].astype(F32), gram_ref[rows])


def sum_coarse_kernel(*refs):
    found = [unpack(ref) for ref in refs[:-1]]
    if len(found) == 4:
        found = [[a + b for a, b in zip(found[k], found[k + 2])] for k in range(2)]
    pack(refs[-1], *[a + b for a, b in zip(*found)])


def coarse_sum(place, mine, theirs):
    per, (rows, lanes) = mine.shape[0] // X, mine.shape[1:]
    shape = (per + 1, rows, lanes)
    scratch = [pltpu.VMEM((rows, lanes), F32)]
    cuts = small(cut_coarse_kernel, (place["x"], mine, swap(theirs, "core")), [shape] * X, 1, BF16, scratch)
    (part,) = small(sum_coarse_kernel, around(cuts, "x"), [shape], 0, BF16)
    (part,) = small(sum_coarse_kernel, (part, swap(part, "near")), [shape], 0, BF16)
    (part,) = small(sum_coarse_kernel, around(part, "far"), [shape], 0, BF16)
    here = around(part, "x")
    return here, [swap(part, "core") for part in here]


def around(value, axis):
    if not isinstance(value, (list, tuple)):
        value = [value] * 4
    return [value[0]] + [lax.ppermute(value[flip], axis, [(i, i ^ flip) for i in range(4)]) for flip in range(1, 4)]


def swap(value, axis):
    return lax.ppermute(value, axis, [(0, 1), (1, 0)])


def all_sum(place, mine, theirs, gradient, error):
    blocks, rows, lanes = mine.shape
    per = blocks // X
    full, half = (per + 1, rows, lanes), (per + 1, rows // 2, lanes)
    cuts = small(cut_kernel, (place["x"], mine, swap(theirs, "core")), [full] * X, 1)
    keep, give = small(halve_kernel, (place["near"], *around(cuts, "x")), [half] * 2, 1)
    (both,) = small(two_kernel, (keep, swap(give, "near")), [half])
    (total,) = small(four_kernel, around(both, "far"), [half])
    rank = 2 * rows
    chunk, gram = small(
        join_kernel, (place["near"], total, swap(total, "near")), [(per, rows, lanes), (rank, rank)], 1
    )
    ready = inverse_and_fetch(gram, gradient, error)
    here = around(chunk, "x")
    first = swap(here[0], "core")
    *ready, here[1], here[2], here[3] = lax.optimization_barrier([*ready, *here[1:]])
    return here, [first] + [swap(part, "core") for part in here[1:]], ready


def whole(first, a, b):
    return jnp.concatenate([jnp.where(first, a, b), jnp.where(first, b, a)], axis=0)


def gather(core_ref, x_ref, refs, u_ref, per):
    first = core_ref[0] == 0
    parts = u_ref.shape[0] // (2 * refs[0].shape[1])
    for flip in range(X):
        owner = x_ref[0] ^ flip
        a_ref, b_ref = refs[flip], refs[X + flip]
        for index in range(per):
            at = pl.ds(pl.multiple_of((owner * per + index) * LANES, LANES), LANES)
            u = whole(first, a_ref[index].astype(F32), b_ref[index].astype(F32))
            u_ref[:, at] = jnp.concatenate(split(u, parts), axis=0)


def left_kernel(core_ref, x_ref, *refs):
    *refs, high_ref, low_ref, t_ref, gram_ref, u_ref, packed_ref = refs
    rows, rank = t_ref.shape
    columns = high_ref.shape[1]
    gather(core_ref, x_ref, refs, u_ref, refs[0].shape[0] - 1)
    u = u_ref[:, :columns]
    t_ref[...] = dot(high_ref[...], u, ((1,), (1,))) + dot(low_ref[...], u, ((1,), (1,)))
    half = packed_ref.shape[0]
    part = half // X
    for flip in range(X):
        at = pl.ds(pl.multiple_of((x_ref[0] ^ flip) * part, part), part)
        packed_ref[at] = unpack(refs[flip])[1]
    gram_ref[:half] = packed_ref[:, :rank]
    gram_ref[half:] = packed_ref[:, rank:]


def left(place, here, there, high, low):
    rows, columns = high.shape
    per, half, _ = here[0].shape
    rank = 2 * half
    return pl.pallas_call(
        left_kernel,
        in_specs=[SMEM] * 2 + [VMEM] * (2 * X + 2),
        out_specs=[VMEM] * 2,
        out_shape=[jax.ShapeDtypeStruct((rows, rank), F32), jax.ShapeDtypeStruct((rank, rank), F32)],
        scratch_shapes=[pltpu.VMEM((rank, X * (per - 1) * LANES), BF16), pltpu.VMEM((half, LANES), F32)],
        compiler_params=params(24),
    )(place["core"], place["x"], *here, *there, high, low)


def lower_inverse(gram):
    rank = gram.shape[0]
    at_row = lax.broadcasted_iota(jnp.int32, (rank, rank), 0)
    at_col = lax.broadcasted_iota(jnp.int32, (rank, rank), 1)
    diagonal = jnp.where(at_row == at_col, gram, 0.0)
    down = lax.rsqrt(jnp.sum(diagonal, axis=1, keepdims=True))
    across = lax.rsqrt(jnp.sum(diagonal, axis=0, keepdims=True))
    work = jnp.concatenate([gram * down * across, jnp.where(at_row == at_col, across, 0.0)], axis=1)
    done = []
    for step in range(0, rank, 2):
        low = step // 8 * 8
        at = step - low
        work = work[at // 8 * 8 :] if at else (work[8:] if step else work)
        one = jnp.broadcast_to(work[:, step : step + 1], work.shape)
        two = jnp.broadcast_to(work[:, step + 1 : step + 2], work.shape)
        first, second = work[at : at + 1], work[at + 1 : at + 2]
        a, b, c = one[at : at + 1], one[at + 1 : at + 2], two[at + 1 : at + 2]
        det = a * c - b * b
        left_over = a * second - b * first
        inverse = 1.0 / det
        done.append((first * lax.rsqrt(a))[:, rank:])
        done.append((left_over * lax.rsqrt(a * det))[:, rank:])
        work = work - (one * ((c * first - b * second) * inverse) + two * (left_over * inverse))
    return jnp.concatenate(done, axis=0)


def inverse_kernel(gram_ref, out_ref):
    out_ref[...] = lower_inverse(gram_ref[...])


def inverse_of(gram):
    return pl.pallas_call(
        inverse_kernel,
        in_specs=[VMEM],
        out_specs=VMEM,
        out_shape=jax.ShapeDtypeStruct(gram.shape, F32),
        compiler_params=params(4),
        cost_estimate=pl.CostEstimate(flops=10_000_000, bytes_accessed=5_000_000, transcendentals=0),
    )(gram)


def fetch_kernel(gram_ref, g_ref, e_ref, out_ref, g_near, e_near, sems):
    copies = [
        pltpu.make_async_copy(far, near, sems.at[index])
        for index, (far, near) in enumerate([(g_ref, g_near), (e_ref, e_near)])
    ]
    for copy in copies:
        copy.start()
    out_ref[...] = lower_inverse(gram_ref[...])
    for copy in copies:
        copy.wait()


def inverse_and_fetch(gram, gradient, error):
    far = pl.BlockSpec(memory_space=pltpu.HBM)
    return pl.pallas_call(
        fetch_kernel,
        in_specs=[VMEM, far, far],
        out_specs=[VMEM] * 3,
        out_shape=[
            jax.ShapeDtypeStruct(gram.shape, F32),
            pltpu.VMEM(gradient.shape, BF16),
            pltpu.VMEM(error.shape, BF16),
        ],
        scratch_shapes=[pltpu.SemaphoreType.DMA((2,))],
        compiler_params=params(24),
        cost_estimate=pl.CostEstimate(flops=10_000_000, bytes_accessed=5_000_000, transcendentals=0),
    )(gram, *in_hbm(gradient, error))


def end_kernel(core_ref, x_ref, *refs):
    *refs, inverse_ref, p_ref, g_ref, e_ref, new_ref, q_ref, u_ref, half_ref = refs
    rank = p_ref.shape[1]
    width = q_ref.shape[1]
    step = pl.program_id(0)

    @pl.when(step == 0)
    def _():
        gather(core_ref, x_ref, refs, u_ref, refs[0].shape[0])
        half_ref[...] = dot(p_ref[...], inverse_ref[...], ((1,), (1,)), HIGH).astype(BF16)

    at = pl.ds(pl.multiple_of(step * width, LANES), width)
    high, mid, low = split(inverse_ref[...], 3)
    q = dot(low, u_ref[:rank, at]) + dot(jnp.concatenate([mid] * 2, axis=1), u_ref[: 2 * rank, at])
    q = dot(jnp.concatenate([high] * 3, axis=1), u_ref[:, at]) + q
    q_ref[...] = q
    for block in range(width // LANES):
        recon = dot(half_ref[...], q[:, block * LANES : (block + 1) * LANES].astype(BF16))
        part = pl.ds(block * LANES, LANES)
        far = pl.ds(pl.multiple_of(step * width + block * LANES, LANES), LANES)
        for replica in range(g_ref.shape[0]):
            corrected = g_ref[replica, :, far] + e_ref[replica, :, far]
            new_ref[replica, :, part] = (corrected.astype(F32) - recon).astype(BF16)


def end(place, here, there, p, inverse, gradient, error, width=1152):
    replicas, rows, columns = gradient.shape
    rank = p.shape[1]
    per = here[0].shape[0]
    wide = pl.BlockSpec((replicas, rows, width), lambda j: (0, 0, j))
    return pl.pallas_call(
        end_kernel,
        grid=(columns // width,),
        in_specs=[SMEM] * 2 + [VMEM] * (2 * X + 4),
        out_specs=[wide, pl.BlockSpec((rank, width), lambda j: (0, j))],
        out_shape=[
            jax.ShapeDtypeStruct(gradient.shape, BF16),
            jax.ShapeDtypeStruct((rank, columns), F32),
        ],
        scratch_shapes=[pltpu.VMEM((3 * rank, X * per * LANES), BF16), pltpu.VMEM((rows, rank), BF16)],
        compiler_params=params(24),
    )(place["core"], place["x"], *here, *there, inverse, p, gradient, error)


def per_device(gradient, error_buffer, q_start):
    place = {axis: lax.axis_index(axis).astype(jnp.int32).reshape(1) for axis in ("x", "near", "core")}
    core = place["core"]
    high, low, term = start(gradient, error_buffer, q_start.T)
    mine, theirs, _ = right(core, around(term, "y"), high, low, kind=BF16)
    here, there = coarse_sum(place, mine, theirs)
    term, gram = left(place, here, there, high, low)
    mine, theirs, p = right(core, around(term, "y"), high, low, inverse_of(gram))
    here, there, ready = all_sum(place, mine, theirs, gradient, error_buffer)
    new_error, q_factor = end(place, here, there, p, *ready)
    return new_error, q_factor.T


def solution(mesh):
    fine = Mesh(mesh.devices.reshape(X, FAR, NEAR, CORES, Y), ("x", "far", "near", "core", "y"))
    rows = ("x", "far", "near", "core")
    return jax.shard_map(
        per_device,
        mesh=fine,
        in_specs=(P(None, rows, "y"), P(None, rows, "y"), P("y", None)),
        out_specs=(P(None, rows, "y"), P("y", None)),
        check_vma=False,
    )
```

```python
import functools

import jax
import jax.numpy as jnp
from jax import lax
from jax.experimental import pallas as pl
from jax.experimental.pallas import tpu as pltpu
from jax.sharding import Mesh
from jax.sharding import PartitionSpec as P

X, FAR, NEAR, CORES, Y = 4, 4, 2, 2, 4
LANES = 128
F32, BF16 = jnp.float32, jnp.bfloat16
HIGH = lax.Precision.HIGHEST
VMEM = pl.BlockSpec(memory_space=pltpu.VMEM)
SMEM = pl.BlockSpec(memory_space=pltpu.SMEM)


def split(value, parts):
    found = []
    for _ in range(parts):
        found.append(value.astype(BF16))
        value = value - found[-1].astype(F32)
    return found


def dot(a, b, contract=((1,), (0,)), precision=None):
    return lax.dot_general(a, b, (contract, ((), ())), precision=precision, preferred_element_type=F32)


def params(mib, **more):
    return pltpu.CompilerParams(vmem_limit_bytes=mib << 20, **more)


def start_kernel(height, x_ref, g_ref, e_ref, q_ref, high_ref, low_ref, p_ref, *refs):
    *piece_refs, g_near, e_near, q_near, sems, q_sem = refs
    replicas, rows, columns = g_ref.shape
    steps = rows // height
    copies = []
    for index in range(steps):
        at = (slice(None), pl.ds(index * height, height))
        copies.append([
            pltpu.make_async_copy(far.at[at], near.at[at], sems.at[which, index])
            for which, (far, near) in enumerate([(g_ref, g_near), (e_ref, e_near)])
        ])
        for copy in copies[-1]:
            copy.start()
        if index == 0:
            q_copy = pltpu.make_async_copy(q_ref, q_near, q_sem)
            q_copy.start()
    for index, pair in enumerate(copies):
        for copy in pair:
            copy.wait()
        row = pl.ds(index * height, height)
        for block in range(columns // LANES):
            at = pl.ds(block * LANES, LANES)
            total = (g_near[0, row, at] + e_near[0, row, at]).astype(F32)
            for replica in range(1, replicas):
                total = total + (g_near[replica, row, at] + e_near[replica, row, at]).astype(F32)
            high_ref[row, at], low_ref[row, at] = split(total * (1.0 / replicas), 2)
        if index >= steps - 2:
            if index == steps - 2:
                q_copy.wait()
                row = pl.ds(0, rows - height)
            both = jnp.concatenate([high_ref[row, :columns], low_ref[row]], axis=0)
            term = dot(both, q_near[...], ((1,), (1,)))
            p_ref[row] = term[: row.size] + term[row.size :]
    high_ref[:, columns:] = jnp.zeros((rows, high_ref.shape[1] - columns), BF16)
    for flip, piece_ref in enumerate(piece_refs):
        width = piece_ref.shape[1]
        piece_ref[...] = high_ref[:, pl.ds(pl.multiple_of((x_ref[0] ^ flip) * width, LANES), width)]


def in_hbm(*values):
    return [pltpu.with_memory_space_constraint(value, pltpu.HBM) for value in values]


def start(place, gradient, error, q_turned, height=16):
    replicas, rows, columns = gradient.shape
    width = -(-columns // (X * LANES)) * LANES
    far = pl.BlockSpec(memory_space=pltpu.HBM)
    return pl.pallas_call(
        functools.partial(start_kernel, height),
        in_specs=[SMEM] + [far] * 3,
        out_specs=[VMEM] * (3 + X),
        out_shape=[
            jax.ShapeDtypeStruct((rows, X * width), BF16),
            jax.ShapeDtypeStruct((rows, columns), BF16),
            jax.ShapeDtypeStruct((rows, q_turned.shape[0]), F32),
        ]
        + [jax.ShapeDtypeStruct((rows, width), BF16)] * X,
        scratch_shapes=[
            pltpu.VMEM(gradient.shape, BF16),
            pltpu.VMEM(error.shape, BF16),
            pltpu.VMEM(q_turned.shape, BF16),
            pltpu.SemaphoreType.DMA((2, rows // height)),
            pltpu.SemaphoreType.DMA,
        ],
        compiler_params=params(24),
    )(place["x"], *in_hbm(gradient, error, q_turned))


def fold(gram):
    half = gram.shape[0] // 2
    return jnp.concatenate([gram[:half], gram[half:]], axis=1)


def right_kernel(blocks, core_ref, own, one, two, three, high_ref, low_ref, mine_ref, theirs_ref):
    p = (own[...] + two[...]) + (one[...] + three[...])
    rank = p.shape[1]
    half = rank // 2
    first = core_ref[0] == 0
    turned = p.T
    stack = jnp.concatenate(split(turned, 3), axis=0)
    for block in range(blocks):
        at = pl.ds(block * LANES, LANES)
        top = dot(stack, high_ref[:, at])
        low = dot(stack[: 2 * rank], low_ref[:, at])
        u = top[:rank] + ((top[rank : 2 * rank] + low[:rank]) + (top[2 * rank :] + low[rank:]))
        mine_ref[block] = jnp.where(first, u[:half], u[half:])
        theirs_ref[block] = jnp.where(first, u[half:], u[:half]).astype(BF16)
    gram = fold(dot(turned, p, ((1,), (0,)), HIGH))
    mine_ref[blocks] = gram
    for index, part in enumerate(split(gram, 3)):
        theirs_ref[blocks + index] = part


def right(place, parts, high, low):
    rank = parts[0].shape[1]
    blocks = low.shape[1] // LANES
    return pl.pallas_call(
        functools.partial(right_kernel, blocks),
        in_specs=[SMEM] + [VMEM] * 6,
        out_specs=[VMEM] * 2,
        out_shape=[
            jax.ShapeDtypeStruct((blocks + 1, rank // 2, LANES), F32),
            jax.ShapeDtypeStruct((blocks + 3, rank // 2, LANES), BF16),
        ],
        compiler_params=params(24),
    )(place["core"], *parts, high, low)


def next_right_kernel(core_ref, x_ref, inverse_ref, *refs):
    *in_refs, mean_ref, mine_ref, theirs_ref, p_ref, all_ref = refs
    first = core_ref[0] == 0
    turned = dot(inverse_ref[...], total_of(in_refs), ((1,), (0,)), HIGH)
    rank = turned.shape[0]
    half = rank // 2
    blocks = mine_ref.shape[0] - 1
    stack = jnp.concatenate(split(turned, 3), axis=0)
    for block in range(blocks):
        top = dot(stack, mean_ref[:, pl.ds(block * LANES, LANES)])
        u = top[:rank] + (top[rank : 2 * rank] + top[2 * rank :])
        mine_ref[block] = jnp.where(first, u[:half], u[half:])
        theirs_ref[block] = jnp.where(first, u[half:], u[:half])
    gram = fold(dot(turned, turned, ((1,), (1,)), HIGH))
    mine_ref[blocks] = gram
    theirs_ref[blocks] = gram
    all_ref[...] = turned.T
    rows = p_ref.shape[0]
    p_ref[...] = all_ref[pl.ds(pl.multiple_of(x_ref[0] * rows, rows), rows)]


def next_right(place, inverse, parts, mean):
    rows, width = mean.shape
    half = inverse.shape[0] // 2
    shape = jax.ShapeDtypeStruct((width // LANES + 1, half, LANES), F32)
    return pl.pallas_call(
        next_right_kernel,
        in_specs=[SMEM] * 2 + [VMEM] * (2 + Y),
        out_specs=[VMEM] * 3,
        out_shape=[shape, shape, jax.ShapeDtypeStruct((rows // X, 2 * half), F32)],
        scratch_shapes=[pltpu.VMEM((rows, 2 * half), F32)],
        compiler_params=params(24),
    )(place["core"], place["x"], inverse, *parts, mean)


def total_of(refs, *at):
    found = [ref[at] if at else ref[...] for ref in refs]
    if len(found) == 4:
        found = [found[0] + found[2], found[1] + found[3]]
    return found[0] + found[1]


def halve_kernel(near_ref, *refs):
    *in_refs, keep_ref, give_ref = refs
    rows = keep_ref.shape[1]
    place = near_ref[0] * rows
    keep_ref[...] = total_of(in_refs, slice(None), pl.ds(pl.multiple_of(place, rows), rows))
    give_ref[...] = total_of(in_refs, slice(None), pl.ds(pl.multiple_of(rows - place, rows), rows))


def sum_kernel(*refs):
    refs[-1][...] = total_of(refs[:-1])


def join_kernel(near_ref, here_ref, there_ref, chunk_ref, gram_ref):
    per, rows = chunk_ref.shape[0], here_ref.shape[1]
    place = near_ref[0] * rows
    chunk_ref[:, pl.ds(pl.multiple_of(place, rows), rows)] = here_ref[:per]
    chunk_ref[:, pl.ds(pl.multiple_of(rows - place, rows), rows)] = there_ref[:per]
    first = near_ref[0] == 0
    here, there = here_ref[per], there_ref[per]
    packed = jnp.concatenate([jnp.where(first, here, there), jnp.where(first, there, here)], axis=0)
    half, rank = packed.shape[0], gram_ref.shape[0]
    gram_ref[:half] = packed[:, :rank]
    gram_ref[half:] = packed[:, rank:]


def small(kernel, operands, shapes, scalars=0, kind=F32, scratch=()):
    return pl.pallas_call(
        kernel,
        in_specs=[SMEM] * scalars + [VMEM] * (len(operands) - scalars),
        out_specs=[VMEM] * len(shapes),
        out_shape=[jax.ShapeDtypeStruct(shape, kind) for shape in shapes],
        scratch_shapes=scratch,
        compiler_params=params(8),
    )(*operands)


def pack(ref, u, gram):
    per = u.shape[0]
    ref[:per] = u.astype(BF16)
    parts = [part.astype(F32) for part in split(gram, 3)]
    spare = ref.shape[1] - 3 * gram.shape[0]
    ref[per] = jnp.concatenate(parts + [jnp.zeros((spare, LANES), F32)], axis=0).astype(BF16)


def unpack(ref):
    per, rows, _ = ref.shape
    block = ref[per - 1].astype(F32)
    part = rows // X
    return ref[: per - 1].astype(F32), block[:part] + (block[part : 2 * part] + block[2 * part : 3 * part])


def cut_coarse_kernel(x_ref, a_ref, b_ref, *refs):
    *out_refs, gram_ref = refs
    last = a_ref.shape[0] - 1
    per = out_refs[0].shape[0] - 1
    part = gram_ref.shape[0] // X
    gram = b_ref[last].astype(F32) + (b_ref[last + 1].astype(F32) + b_ref[last + 2].astype(F32))
    gram_ref[...] = a_ref[last] + gram
    for flip, out_ref in enumerate(out_refs):
        owner = x_ref[0] ^ flip
        at = pl.ds(owner * per, per)
        rows = pl.ds(pl.multiple_of(owner * part, part), part)
        pack(out_ref, a_ref[at] + b_ref[at].astype(F32), gram_ref[rows])


def sum_coarse_kernel(*refs):
    found = [unpack(ref) for ref in refs[:-1]]
    if len(found) == 4:
        found = [[a + b for a, b in zip(found[k], found[k + 2])] for k in range(2)]
    pack(refs[-1], *[a + b for a, b in zip(*found)])


def coarse_sum(place, mine, theirs):
    per, (rows, lanes) = mine.shape[0] // X, mine.shape[1:]
    shape = (per + 1, rows, lanes)
    scratch = [pltpu.VMEM((rows, lanes), F32)]
    cuts = small(cut_coarse_kernel, (place["x"], mine, swap(theirs, "core")), [shape] * X, 1, BF16, scratch)
    (part,) = small(sum_coarse_kernel, around(cuts, "x"), [shape], 0, BF16)
    (part,) = small(sum_coarse_kernel, (part, swap(part, "near")), [shape], 0, BF16)
    (part,) = small(sum_coarse_kernel, around(part, "far"), [shape], 0, BF16)
    return part


def around(value, axis):
    if not isinstance(value, (list, tuple)):
        value = [value] * 4
    return [value[0]] + [lax.ppermute(value[flip], axis, [(i, i ^ flip) for i in range(4)]) for flip in range(1, 4)]


def swap(value, axis):
    return lax.ppermute(value, axis, [(0, 1), (1, 0)])


def all_sum(place, mine, theirs, gradient, error):
    blocks, rows, lanes = mine.shape
    half = (blocks, rows // 2, lanes)
    keep, give = small(halve_kernel, (place["near"], mine, swap(theirs, "core")), [half] * 2, 1)
    (both,) = small(sum_kernel, (keep, swap(give, "near")), [half])
    (total,) = small(sum_kernel, around(both, "far"), [half])
    rank = 2 * rows
    chunk, gram = small(
        join_kernel, (place["near"], total, swap(total, "near")), [(blocks - 1, rows, lanes), (rank, rank)], 1
    )
    ready = inverse_and_fetch(gram, gradient, error)
    here = around(chunk, "x")
    first = swap(here[0], "core")
    *ready, here[1], here[2], here[3] = lax.optimization_barrier([*ready, *here[1:]])
    return here, [first] + [swap(part, "core") for part in here[1:]], ready


def whole(first, a, b):
    return jnp.concatenate([jnp.where(first, a, b), jnp.where(first, b, a)], axis=0)


def gather(core_ref, x_ref, refs, u_ref, per):
    first = core_ref[0] == 0
    parts = u_ref.shape[0] // (2 * refs[0].shape[1])
    for flip in range(X):
        owner = x_ref[0] ^ flip
        a_ref, b_ref = refs[flip], refs[X + flip]
        for index in range(per):
            at = pl.ds(pl.multiple_of((owner * per + index) * LANES, LANES), LANES)
            u = whole(first, a_ref[index].astype(F32), b_ref[index].astype(F32))
            u_ref[:, at] = jnp.concatenate(split(u, parts), axis=0)


def left_kernel(core_ref, x_ref, part_ref, other_ref, *refs):
    *piece_refs, mean_ref, out_ref = refs
    height = piece_refs[0].shape[0]
    for flip, piece_ref in enumerate(piece_refs):
        mean_ref[pl.ds(pl.multiple_of((x_ref[0] ^ flip) * height, height), height)] = piece_ref[...]
    per = part_ref.shape[0] - 1
    first = core_ref[0] == 0
    u = jnp.concatenate([whole(first, part_ref[block], other_ref[block]) for block in range(per)], axis=1)
    rows = mean_ref.shape[0]
    out_ref[:, :rows] = dot(u, mean_ref[...], ((1,), (1,)))
    quarter = unpack(part_ref)[1]
    side = quarter.shape[1] // 2
    quarter = jnp.concatenate([quarter[:, :side], quarter[:, side:]], axis=0)
    spare = out_ref.shape[0] - quarter.shape[0]
    out_ref[:, rows:] = jnp.concatenate([quarter, jnp.zeros((spare, side), F32)], axis=0)


def left(place, part, pieces):
    height, width = pieces[0].shape
    rows = X * height
    half, lanes = part.shape[1:]
    return pl.pallas_call(
        left_kernel,
        in_specs=[SMEM] * 2 + [VMEM] * (2 + X),
        out_specs=[VMEM] * 2,
        out_shape=[
            jax.ShapeDtypeStruct((rows, width), BF16),
            jax.ShapeDtypeStruct((2 * half, rows + lanes // 2), F32),
        ],
        compiler_params=params(24),
    )(place["core"], place["x"], part, swap(part, "core"), *pieces)


def left_sum_kernel(x_ref, *refs):
    *in_refs, t_ref, gram_ref = refs
    rows = t_ref.shape[1]
    t_ref[...] = total_of(in_refs, slice(None), slice(0, rows))
    half = gram_ref.shape[0] // 2
    part = half // X
    for flip, in_ref in enumerate(in_refs):
        quarter = in_ref[: 2 * part, rows:]
        place = (x_ref[0] ^ flip) * part
        gram_ref[pl.ds(pl.multiple_of(place, part), part)] = quarter[:part]
        gram_ref[pl.ds(pl.multiple_of(half + place, part), part)] = quarter[part:]


def lower_inverse(gram):
    rank = gram.shape[0]
    at_row = lax.broadcasted_iota(jnp.int32, (rank, rank), 0)
    at_col = lax.broadcasted_iota(jnp.int32, (rank, rank), 1)
    diagonal = jnp.where(at_row == at_col, gram, 0.0)
    down = lax.rsqrt(jnp.sum(diagonal, axis=1, keepdims=True))
    across = lax.rsqrt(jnp.sum(diagonal, axis=0, keepdims=True))
    work = jnp.concatenate([gram * down * across, jnp.where(at_row == at_col, across, 0.0)], axis=1)
    done = []
    for step in range(0, rank, 2):
        low = step // 8 * 8
        at = step - low
        work = work[at // 8 * 8 :] if at else (work[8:] if step else work)
        one = jnp.broadcast_to(work[:, step : step + 1], work.shape)
        two = jnp.broadcast_to(work[:, step + 1 : step + 2], work.shape)
        first, second = work[at : at + 1], work[at + 1 : at + 2]
        a, b, c = one[at : at + 1], one[at + 1 : at + 2], two[at + 1 : at + 2]
        det = a * c - b * b
        left_over = a * second - b * first
        inverse = 1.0 / det
        done.append((first * lax.rsqrt(a))[:, rank:])
        done.append((left_over * lax.rsqrt(a * det))[:, rank:])
        work = work - (one * ((c * first - b * second) * inverse) + two * (left_over * inverse))
    return jnp.concatenate(done, axis=0)


def inverse_kernel(gram_ref, out_ref):
    out_ref[...] = lower_inverse(gram_ref[...])


def inverse_of(gram):
    return pl.pallas_call(
        inverse_kernel,
        in_specs=[VMEM],
        out_specs=VMEM,
        out_shape=jax.ShapeDtypeStruct(gram.shape, F32),
        compiler_params=params(4),
        cost_estimate=pl.CostEstimate(flops=10_000_000, bytes_accessed=5_000_000, transcendentals=0),
    )(gram)


def fetch_kernel(gram_ref, g_ref, e_ref, out_ref, g_near, e_near, sems):
    copies = [
        pltpu.make_async_copy(far, near, sems.at[index])
        for index, (far, near) in enumerate([(g_ref, g_near), (e_ref, e_near)])
    ]
    for copy in copies:
        copy.start()
    out_ref[...] = lower_inverse(gram_ref[...])
    for copy in copies:
        copy.wait()


def inverse_and_fetch(gram, gradient, error):
    far = pl.BlockSpec(memory_space=pltpu.HBM)
    return pl.pallas_call(
        fetch_kernel,
        in_specs=[VMEM, far, far],
        out_specs=[VMEM] * 3,
        out_shape=[
            jax.ShapeDtypeStruct(gram.shape, F32),
            pltpu.VMEM(gradient.shape, BF16),
            pltpu.VMEM(error.shape, BF16),
        ],
        scratch_shapes=[pltpu.SemaphoreType.DMA((2,))],
        compiler_params=params(24),
        cost_estimate=pl.CostEstimate(flops=10_000_000, bytes_accessed=5_000_000, transcendentals=0),
    )(gram, *in_hbm(gradient, error))


def end_kernel(core_ref, x_ref, *refs):
    *refs, inverse_ref, p_ref, g_ref, e_ref, new_ref, q_ref, u_ref, half_ref = refs
    rank = p_ref.shape[1]
    width = q_ref.shape[1]
    step = pl.program_id(0)

    @pl.when(step == 0)
    def _():
        gather(core_ref, x_ref, refs, u_ref, refs[0].shape[0])
        half_ref[...] = dot(p_ref[...], inverse_ref[...], ((1,), (1,)), HIGH).astype(BF16)

    at = pl.ds(pl.multiple_of(step * width, LANES), width)
    high, mid, low = split(inverse_ref[...], 3)
    q = dot(low, u_ref[:rank, at]) + dot(jnp.concatenate([mid] * 2, axis=1), u_ref[: 2 * rank, at])
    q = dot(jnp.concatenate([high] * 3, axis=1), u_ref[:, at]) + q
    q_ref[...] = q
    for block in range(width // LANES):
        recon = dot(half_ref[...], q[:, block * LANES : (block + 1) * LANES].astype(BF16))
        part = pl.ds(block * LANES, LANES)
        far = pl.ds(pl.multiple_of(step * width + block * LANES, LANES), LANES)
        for replica in range(g_ref.shape[0]):
            corrected = g_ref[replica, :, far] + e_ref[replica, :, far]
            new_ref[replica, :, part] = (corrected.astype(F32) - recon).astype(BF16)


def end(place, here, there, p, inverse, gradient, error, width=1152):
    replicas, rows, columns = gradient.shape
    rank = p.shape[1]
    per = here[0].shape[0]
    wide = pl.BlockSpec((replicas, rows, width), lambda j: (0, 0, j))
    return pl.pallas_call(
        end_kernel,
        grid=(columns // width,),
        in_specs=[SMEM] * 2 + [VMEM] * (2 * X + 4),
        out_specs=[wide, pl.BlockSpec((rank, width), lambda j: (0, j))],
        out_shape=[
            jax.ShapeDtypeStruct(gradient.shape, BF16),
            jax.ShapeDtypeStruct((rank, columns), F32),
        ],
        scratch_shapes=[pltpu.VMEM((3 * rank, X * per * LANES), BF16), pltpu.VMEM((rows, rank), BF16)],
        compiler_params=params(24),
    )(place["core"], place["x"], *here, *there, inverse, p, gradient, error)


def per_device(gradient, error_buffer, q_start):
    place = {axis: lax.axis_index(axis).astype(jnp.int32).reshape(1) for axis in ("x", "near", "core")}
    high, low, term, *pieces = start(place, gradient, error_buffer, q_start.T)
    parts = around(term, "y")
    pieces = around(pieces, "x")
    part = coarse_sum(place, *right(place, parts, high, low))
    mean, term = left(place, part, pieces)
    rank, width = term.shape
    term, gram = small(
        left_sum_kernel, (place["x"], *around(term, "x")), [(rank, width - rank), (rank, rank)], 1
    )
    mine, theirs, p = next_right(place, inverse_of(gram), around(term, "y"), mean)
    here, there, ready = all_sum(place, mine, theirs, gradient, error_buffer)
    new_error, q_factor = end(place, here, there, p, *ready)
    return new_error, q_factor.T


def solution(mesh):
    fine = Mesh(mesh.devices.reshape(X, FAR, NEAR, CORES, Y), ("x", "far", "near", "core", "y"))
    rows = ("x", "far", "near", "core")
    return jax.shard_map(
        per_device,
        mesh=fine,
        in_specs=(P(None, rows, "y"), P(None, rows, "y"), P("y", None)),
        out_specs=(P(None, rows, "y"), P("y", None)),
        check_vma=False,
    )
```

```python
import functools

import jax
import jax.numpy as jnp
from jax import lax
from jax.experimental import pallas as pl
from jax.experimental.pallas import tpu as pltpu
from jax.sharding import Mesh
from jax.sharding import PartitionSpec as P

X, FAR, NEAR, CORES, Y = 4, 4, 2, 2, 4
LANES = 128
SENT, SHARED = (0, 2, 1, 3), (0, 1, 3, 2)
F32, BF16 = jnp.float32, jnp.bfloat16
HIGH = lax.Precision.HIGHEST
VMEM = pl.BlockSpec(memory_space=pltpu.VMEM)
SMEM = pl.BlockSpec(memory_space=pltpu.SMEM)


def split(value, parts):
    found = []
    for _ in range(parts):
        found.append(value.astype(BF16))
        value = value - found[-1].astype(F32)
    return found


def dot(a, b, contract=((1,), (0,)), precision=None):
    return lax.dot_general(a, b, (contract, ((), ())), precision=precision, preferred_element_type=F32)


def params(mib, **more):
    return pltpu.CompilerParams(vmem_limit_bytes=mib << 20, **more)


def start_kernel(height, x_ref, g_ref, e_ref, q_ref, high_ref, p_ref, *refs):
    *piece_refs, g_near, e_near, q_near, sems, q_sem = refs
    replicas, rows, columns = g_ref.shape
    steps = rows // height
    copies = []
    for index in range(steps):
        at = (slice(None), pl.ds(index * height, height))
        copies.append([
            pltpu.make_async_copy(far.at[at], near.at[at], sems.at[which, index])
            for which, (far, near) in enumerate([(g_ref, g_near), (e_ref, e_near)])
        ])
        for copy in copies[-1]:
            copy.start()
        if index == 0:
            q_copy = pltpu.make_async_copy(q_ref, q_near, q_sem)
            q_copy.start()
    for index, pair in enumerate(copies):
        for copy in pair:
            copy.wait()
        row = pl.ds(index * height, height)
        for block in range(columns // LANES):
            at = pl.ds(block * LANES, LANES)
            total = (g_near[0, row, at] + e_near[0, row, at]).astype(F32)
            for replica in range(1, replicas):
                total = total + (g_near[replica, row, at] + e_near[replica, row, at]).astype(F32)
            high_ref[row, at] = (total * (1.0 / replicas)).astype(BF16)
        if index >= steps - 2:
            if index == steps - 2:
                q_copy.wait()
                row = pl.ds(0, rows - height)
            p_ref[row] = dot(high_ref[row, :columns], q_near[...], ((1,), (1,)))
    high_ref[:, columns:] = jnp.zeros((rows, high_ref.shape[1] - columns), BF16)
    for flip, piece_ref in enumerate(piece_refs):
        width = piece_ref.shape[1]
        piece_ref[...] = high_ref[:, pl.ds(pl.multiple_of((x_ref[0] ^ flip) * width, LANES), width)]


def in_hbm(*values):
    return [pltpu.with_memory_space_constraint(value, pltpu.HBM) for value in values]


def start(place, gradient, error, q_turned, height=16):
    replicas, rows, columns = gradient.shape
    width = -(-columns // (X * LANES)) * LANES
    far = pl.BlockSpec(memory_space=pltpu.HBM)
    return pl.pallas_call(
        functools.partial(start_kernel, height),
        in_specs=[SMEM] + [far] * 3,
        out_specs=[VMEM] * (2 + X),
        out_shape=[
            jax.ShapeDtypeStruct((rows, X * width), BF16),
            jax.ShapeDtypeStruct((rows, q_turned.shape[0]), F32),
        ]
        + [jax.ShapeDtypeStruct((rows, width), BF16)] * X,
        scratch_shapes=[
            pltpu.VMEM(gradient.shape, BF16),
            pltpu.VMEM(error.shape, BF16),
            pltpu.VMEM(q_turned.shape, BF16),
            pltpu.SemaphoreType.DMA((2, rows // height)),
            pltpu.SemaphoreType.DMA,
        ],
        compiler_params=params(24),
    )(place["x"], *in_hbm(gradient, error, q_turned))


def fold(gram):
    half = gram.shape[0] // 2
    return jnp.concatenate([gram[:half], gram[half:]], axis=1)


def right_kernel(blocks, core_ref, own, one, two, three, high_ref, mine_ref, theirs_ref):
    p = total_of([own, one, two, three])
    rank = p.shape[1]
    half = rank // 2
    first = core_ref[0] == 0
    turned = p.T
    stack = jnp.concatenate(split(turned, 3), axis=0)
    for block in range(blocks):
        at = pl.ds(block * LANES, LANES)
        top = dot(stack, high_ref[:, at])
        u = top[:rank] + (top[rank : 2 * rank] + top[2 * rank :])
        mine_ref[block] = jnp.where(first, u[:half], u[half:])
        theirs_ref[block] = jnp.where(first, u[half:], u[:half]).astype(BF16)
    gram = fold(dot(turned, p, ((1,), (0,)), HIGH))
    mine_ref[blocks] = gram
    for index, part in enumerate(split(gram, 3)):
        theirs_ref[blocks + index] = part


def right(place, parts, high, columns):
    rank = parts[0].shape[1]
    blocks = columns // LANES
    return pl.pallas_call(
        functools.partial(right_kernel, blocks),
        in_specs=[SMEM] + [VMEM] * 5,
        out_specs=[VMEM] * 2,
        out_shape=[
            jax.ShapeDtypeStruct((blocks + 1, rank // 2, LANES), F32),
            jax.ShapeDtypeStruct((blocks + 3, rank // 2, LANES), BF16),
        ],
        compiler_params=params(24),
    )(place["core"], *parts, high)


def next_right_kernel(core_ref, x_ref, inverse_ref, *refs):
    *in_refs, mean_ref, mine_ref, theirs_ref, p_ref, all_ref = refs
    first = core_ref[0] == 0
    turned = dot(inverse_ref[...], total_of(in_refs), ((1,), (0,)), HIGH)
    rank = turned.shape[0]
    half = rank // 2
    blocks = mine_ref.shape[0] - 1
    stack = jnp.concatenate(split(turned, 3), axis=0)
    for block in range(blocks):
        top = dot(stack, mean_ref[:, pl.ds(block * LANES, LANES)])
        u = top[:rank] + (top[rank : 2 * rank] + top[2 * rank :])
        mine_ref[block] = jnp.where(first, u[:half], u[half:])
        theirs_ref[block] = jnp.where(first, u[half:], u[:half])
    gram = fold(dot(turned, turned, ((1,), (1,)), HIGH))
    mine_ref[blocks] = gram
    theirs_ref[blocks] = gram
    all_ref[...] = turned.T
    rows = p_ref.shape[0]
    p_ref[...] = all_ref[pl.ds(pl.multiple_of(x_ref[0] * rows, rows), rows)]


def next_right(place, inverse, parts, mean):
    rows, width = mean.shape
    half = inverse.shape[0] // 2
    shape = jax.ShapeDtypeStruct((width // LANES + 1, half, LANES), F32)
    return pl.pallas_call(
        next_right_kernel,
        in_specs=[SMEM] * 2 + [VMEM] * (2 + Y),
        out_specs=[VMEM] * 3,
        out_shape=[shape, shape, jax.ShapeDtypeStruct((rows // X, 2 * half), F32)],
        scratch_shapes=[pltpu.VMEM((rows, 2 * half), F32)],
        compiler_params=params(24),
    )(place["core"], place["x"], inverse, *parts, mean)


def total_of(refs, *at):
    found = [ref[at] if at else ref[...] for ref in refs]
    if len(found) == 4:
        found = [found[0] + found[3], found[1] + found[2]]
    return found[0] + found[1]


def halve_kernel(near_ref, *refs):
    *in_refs, keep_ref, give_ref = refs
    rows = keep_ref.shape[1]
    place = near_ref[0] * rows
    keep_ref[...] = total_of(in_refs, slice(None), pl.ds(pl.multiple_of(place, rows), rows))
    give_ref[...] = total_of(in_refs, slice(None), pl.ds(pl.multiple_of(rows - place, rows), rows))


def sum_kernel(*refs):
    refs[-1][...] = total_of(refs[:-1])


def join_kernel(near_ref, here_ref, there_ref, chunk_ref, gram_ref):
    per, rows = chunk_ref.shape[0], here_ref.shape[1]
    place = near_ref[0] * rows
    chunk_ref[:, pl.ds(pl.multiple_of(place, rows), rows)] = here_ref[:per]
    chunk_ref[:, pl.ds(pl.multiple_of(rows - place, rows), rows)] = there_ref[:per]
    first = near_ref[0] == 0
    here, there = here_ref[per], there_ref[per]
    packed = jnp.concatenate([jnp.where(first, here, there), jnp.where(first, there, here)], axis=0)
    half, rank = packed.shape[0], gram_ref.shape[0]
    gram_ref[:half] = packed[:, :rank]
    gram_ref[half:] = packed[:, rank:]


def small(kernel, operands, shapes, scalars=0, kind=F32, scratch=()):
    return pl.pallas_call(
        kernel,
        in_specs=[SMEM] * scalars + [VMEM] * (len(operands) - scalars),
        out_specs=[VMEM] * len(shapes),
        out_shape=[jax.ShapeDtypeStruct(shape, kind) for shape in shapes],
        scratch_shapes=scratch,
        compiler_params=params(8),
    )(*operands)


def pack(ref, u, gram):
    per = u.shape[0]
    ref[:per] = u.astype(BF16)
    parts = [part.astype(F32) for part in split(gram, 3)]
    spare = ref.shape[1] - 3 * gram.shape[0]
    ref[per] = jnp.concatenate(parts + [jnp.zeros((spare, LANES), F32)], axis=0).astype(BF16)


def unpack(ref):
    per, rows, _ = ref.shape
    block = ref[per - 1].astype(F32)
    part = rows // X
    return ref[: per - 1].astype(F32), block[:part] + (block[part : 2 * part] + block[2 * part : 3 * part])


def cut_coarse_kernel(x_ref, a_ref, b_ref, *refs):
    *out_refs, gram_ref = refs
    last = a_ref.shape[0] - 1
    per = out_refs[0].shape[0] - 1
    part = gram_ref.shape[0] // X
    gram = b_ref[last].astype(F32) + (b_ref[last + 1].astype(F32) + b_ref[last + 2].astype(F32))
    gram_ref[...] = a_ref[last] + gram
    for flip, out_ref in enumerate(out_refs):
        owner = x_ref[0] ^ flip
        at = pl.ds(owner * per, per)
        rows = pl.ds(pl.multiple_of(owner * part, part), part)
        pack(out_ref, a_ref[at] + b_ref[at].astype(F32), gram_ref[rows])


def sum_coarse_kernel(*refs):
    found = [unpack(ref) for ref in refs[:-1]]
    if len(found) == 4:
        found = [[a + b for a, b in zip(found[k], found[3 - k])] for k in range(2)]
    pack(refs[-1], *[a + b for a, b in zip(*found)])


def coarse_sum(place, mine, theirs):
    per, (rows, lanes) = mine.shape[0] // X, mine.shape[1:]
    shape = (per + 1, rows, lanes)
    scratch = [pltpu.VMEM((rows, lanes), F32)]
    cuts = small(cut_coarse_kernel, (place["x"], mine, swap(theirs, "core")), [shape] * X, 1, BF16, scratch)
    (part,) = small(sum_coarse_kernel, around(cuts, "x"), [shape], 0, BF16)
    (part,) = small(sum_coarse_kernel, (part, swap(part, "near")), [shape], 0, BF16)
    (part,) = small(sum_coarse_kernel, around(part, "far"), [shape], 0, BF16)
    return part


def around(value, axis):
    if isinstance(value, (list, tuple)):
        return [value[0]] + [flipped(value[flip], axis, flip) for flip in SENT[1:]]
    return [value] + [flipped(value, axis, flip) for flip in SHARED[1:]]


def flipped(value, axis, flip):
    return lax.ppermute(value, axis, [(i, i ^ flip) for i in range(4)])


def swap(value, axis):
    return lax.ppermute(value, axis, [(0, 1), (1, 0)])


def all_sum(place, mine, theirs, gradient, error):
    blocks, rows, lanes = mine.shape
    half = (blocks, rows // 2, lanes)
    keep, give = small(halve_kernel, (place["near"], mine, swap(theirs, "core")), [half] * 2, 1)
    (both,) = small(sum_kernel, (keep, swap(give, "near")), [half])
    (total,) = small(sum_kernel, around(both, "far"), [half])
    rank = 2 * rows
    chunk, gram = small(
        join_kernel, (place["near"], total, swap(total, "near")), [(blocks - 1, rows, lanes), (rank, rank)], 1
    )
    ready = inverse_and_fetch(gram, gradient, error)
    here = around(chunk, "x")
    first = swap(here[0], "core")
    *ready, here[1], here[2], here[3] = lax.optimization_barrier([*ready, *here[1:]])
    return here, [first] + [swap(part, "core") for part in here[1:]], ready


def whole(first, a, b):
    return jnp.concatenate([jnp.where(first, a, b), jnp.where(first, b, a)], axis=0)


def gather(core_ref, x_ref, refs, u_ref, per):
    first = core_ref[0] == 0
    parts = u_ref.shape[0] // (2 * refs[0].shape[1])
    for flip, a_ref, b_ref in zip(SHARED, refs[:X], refs[X:]):
        owner = x_ref[0] ^ flip
        for index in range(per):
            at = pl.ds(pl.multiple_of((owner * per + index) * LANES, LANES), LANES)
            u = whole(first, a_ref[index].astype(F32), b_ref[index].astype(F32))
            u_ref[:, at] = jnp.concatenate(split(u, parts), axis=0)


def left_kernel(core_ref, x_ref, part_ref, other_ref, *refs):
    *piece_refs, mean_ref, out_ref = refs
    height = piece_refs[0].shape[0]
    for flip, piece_ref in zip(SENT, piece_refs):
        mean_ref[pl.ds(pl.multiple_of((x_ref[0] ^ flip) * height, height), height)] = piece_ref[...]
    per = part_ref.shape[0] - 1
    first = core_ref[0] == 0
    u = jnp.concatenate([whole(first, part_ref[block], other_ref[block]) for block in range(per)], axis=1)
    rows = mean_ref.shape[0]
    out_ref[:, :rows] = dot(u, mean_ref[...], ((1,), (1,)))
    quarter = unpack(part_ref)[1]
    side = quarter.shape[1] // 2
    quarter = jnp.concatenate([quarter[:, :side], quarter[:, side:]], axis=0)
    spare = out_ref.shape[0] - quarter.shape[0]
    out_ref[:, rows:] = jnp.concatenate([quarter, jnp.zeros((spare, side), F32)], axis=0)


def left(place, part, pieces):
    height, width = pieces[0].shape
    rows = X * height
    half, lanes = part.shape[1:]
    return pl.pallas_call(
        left_kernel,
        in_specs=[SMEM] * 2 + [VMEM] * (2 + X),
        out_specs=[VMEM] * 2,
        out_shape=[
            jax.ShapeDtypeStruct((rows, width), BF16),
            jax.ShapeDtypeStruct((2 * half, rows + lanes // 2), F32),
        ],
        compiler_params=params(24),
    )(place["core"], place["x"], part, swap(part, "core"), *pieces)


def left_sum_kernel(x_ref, *refs):
    *in_refs, t_ref, gram_ref = refs
    rows = t_ref.shape[1]
    t_ref[...] = total_of(in_refs, slice(None), slice(0, rows))
    half = gram_ref.shape[0] // 2
    part = half // X
    for flip, in_ref in zip(SHARED, in_refs):
        quarter = in_ref[: 2 * part, rows:]
        place = (x_ref[0] ^ flip) * part
        gram_ref[pl.ds(pl.multiple_of(place, part), part)] = quarter[:part]
        gram_ref[pl.ds(pl.multiple_of(half + place, part), part)] = quarter[part:]


def lower_inverse(gram):
    rank = gram.shape[0]
    at_row = lax.broadcasted_iota(jnp.int32, (rank, rank), 0)
    at_col = lax.broadcasted_iota(jnp.int32, (rank, rank), 1)
    diagonal = jnp.where(at_row == at_col, gram, 0.0)
    down = lax.rsqrt(jnp.sum(diagonal, axis=1, keepdims=True))
    across = lax.rsqrt(jnp.sum(diagonal, axis=0, keepdims=True))
    work = jnp.concatenate([gram * down * across, jnp.where(at_row == at_col, across, 0.0)], axis=1)
    done = []
    for step in range(0, rank, 2):
        low = step // 8 * 8
        at = step - low
        work = work[at // 8 * 8 :] if at else (work[8:] if step else work)
        one = jnp.broadcast_to(work[:, step : step + 1], work.shape)
        two = jnp.broadcast_to(work[:, step + 1 : step + 2], work.shape)
        first, second = work[at : at + 1], work[at + 1 : at + 2]
        a, b, c = one[at : at + 1], one[at + 1 : at + 2], two[at + 1 : at + 2]
        det = a * c - b * b
        left_over = a * second - b * first
        inverse = 1.0 / det
        done.append((first * lax.rsqrt(a))[:, rank:])
        done.append((left_over * lax.rsqrt(a * det))[:, rank:])
        work = work - (one * ((c * first - b * second) * inverse) + two * (left_over * inverse))
    return jnp.concatenate(done, axis=0)


def inverse_kernel(gram_ref, out_ref):
    out_ref[...] = lower_inverse(gram_ref[...])


def inverse_of(gram):
    return pl.pallas_call(
        inverse_kernel,
        in_specs=[VMEM],
        out_specs=VMEM,
        out_shape=jax.ShapeDtypeStruct(gram.shape, F32),
        compiler_params=params(4),
        cost_estimate=pl.CostEstimate(flops=10_000_000, bytes_accessed=5_000_000, transcendentals=0),
    )(gram)


def fetch_kernel(gram_ref, g_ref, e_ref, out_ref, g_near, e_near, sems):
    copies = [
        pltpu.make_async_copy(far, near, sems.at[index])
        for index, (far, near) in enumerate([(g_ref, g_near), (e_ref, e_near)])
    ]
    for copy in copies:
        copy.start()
    out_ref[...] = lower_inverse(gram_ref[...])
    for copy in copies:
        copy.wait()


def inverse_and_fetch(gram, gradient, error):
    far = pl.BlockSpec(memory_space=pltpu.HBM)
    return pl.pallas_call(
        fetch_kernel,
        in_specs=[VMEM, far, far],
        out_specs=[VMEM] * 3,
        out_shape=[
            jax.ShapeDtypeStruct(gram.shape, F32),
            pltpu.VMEM(gradient.shape, BF16),
            pltpu.VMEM(error.shape, BF16),
        ],
        scratch_shapes=[pltpu.SemaphoreType.DMA((2,))],
        compiler_params=params(24),
        cost_estimate=pl.CostEstimate(flops=10_000_000, bytes_accessed=5_000_000, transcendentals=0),
    )(gram, *in_hbm(gradient, error))


def end_kernel(core_ref, x_ref, *refs):
    *refs, inverse_ref, p_ref, g_ref, e_ref, new_ref, q_ref, u_ref, half_ref = refs
    rank = p_ref.shape[1]
    width = q_ref.shape[1]
    step = pl.program_id(0)

    @pl.when(step == 0)
    def _():
        gather(core_ref, x_ref, refs, u_ref, refs[0].shape[0])
        half_ref[...] = dot(p_ref[...], inverse_ref[...], ((1,), (1,)), HIGH).astype(BF16)

    at = pl.ds(pl.multiple_of(step * width, LANES), width)
    high, mid, low = split(inverse_ref[...], 3)
    q = dot(low, u_ref[:rank, at]) + dot(jnp.concatenate([mid] * 2, axis=1), u_ref[: 2 * rank, at])
    q = dot(jnp.concatenate([high] * 3, axis=1), u_ref[:, at]) + q
    q_ref[...] = q
    for block in range(width // LANES):
        recon = dot(half_ref[...], q[:, block * LANES : (block + 1) * LANES].astype(BF16))
        part = pl.ds(block * LANES, LANES)
        far = pl.ds(pl.multiple_of(step * width + block * LANES, LANES), LANES)
        for replica in range(g_ref.shape[0]):
            corrected = g_ref[replica, :, far] + e_ref[replica, :, far]
            new_ref[replica, :, part] = (corrected.astype(F32) - recon).astype(BF16)


def end(place, here, there, p, inverse, gradient, error, width=1152):
    replicas, rows, columns = gradient.shape
    rank = p.shape[1]
    per = here[0].shape[0]
    wide = pl.BlockSpec((replicas, rows, width), lambda j: (0, 0, j))
    return pl.pallas_call(
        end_kernel,
        grid=(columns // width,),
        in_specs=[SMEM] * 2 + [VMEM] * (2 * X + 4),
        out_specs=[wide, pl.BlockSpec((rank, width), lambda j: (0, j))],
        out_shape=[
            jax.ShapeDtypeStruct(gradient.shape, BF16),
            jax.ShapeDtypeStruct((rank, columns), F32),
        ],
        scratch_shapes=[pltpu.VMEM((3 * rank, X * per * LANES), BF16), pltpu.VMEM((rows, rank), BF16)],
        compiler_params=params(24),
    )(place["core"], place["x"], *here, *there, inverse, p, gradient, error)


def per_device(gradient, error_buffer, q_start):
    place = {axis: lax.axis_index(axis).astype(jnp.int32).reshape(1) for axis in ("x", "near", "core")}
    high, term, *pieces = start(place, gradient, error_buffer, q_start.T)
    parts = around(term, "y")
    pieces = around(pieces, "x")
    part = coarse_sum(place, *right(place, parts, high, gradient.shape[2]))
    mean, term = left(place, part, pieces)
    rank, width = term.shape
    term, gram = small(
        left_sum_kernel, (place["x"], *around(term, "x")), [(rank, width - rank), (rank, rank)], 1
    )
    mine, theirs, p = next_right(place, inverse_of(gram), around(term, "y"), mean)
    here, there, ready = all_sum(place, mine, theirs, gradient, error_buffer)
    new_error, q_factor = end(place, here, there, p, *ready)
    return new_error, q_factor.T


def solution(mesh):
    fine = Mesh(mesh.devices.reshape(X, FAR, NEAR, CORES, Y), ("x", "far", "near", "core", "y"))
    rows = ("x", "far", "near", "core")
    return jax.shard_map(
        per_device,
        mesh=fine,
        in_specs=(P(None, rows, "y"), P(None, rows, "y"), P("y", None)),
        out_specs=(P(None, rows, "y"), P("y", None)),
        check_vma=False,
    )
```

```python
import functools

import jax
import jax.numpy as jnp
from jax import lax
from jax.experimental import pallas as pl
from jax.experimental.pallas import tpu as pltpu
from jax.sharding import Mesh
from jax.sharding import PartitionSpec as P

X, FAR, NEAR, CORES, Y = 4, 4, 2, 2, 4
LANES = 128
SENT, SHARED = (0, 2, 1, 3), (0, 1, 3, 2)
F32, BF16 = jnp.float32, jnp.bfloat16
HIGH = lax.Precision.HIGHEST
VMEM = pl.BlockSpec(memory_space=pltpu.VMEM)
SMEM = pl.BlockSpec(memory_space=pltpu.SMEM)


def split(value, parts):
    found = []
    for _ in range(parts):
        found.append(value.astype(BF16))
        value = value - found[-1].astype(F32)
    return found


def dot(a, b, contract=((1,), (0,)), precision=None):
    return lax.dot_general(a, b, (contract, ((), ())), precision=precision, preferred_element_type=F32)


def fold(value):
    half = value.shape[0] // 2
    return jnp.concatenate([value[:half], value[half:]], axis=1)


def unfold(value):
    half = value.shape[1] // 2
    return jnp.concatenate([value[:, :half], value[:, half:]], axis=0)


def params(mib, **more):
    return pltpu.CompilerParams(vmem_limit_bytes=mib << 20, **more)


def start_kernel(height, x_ref, g_ref, e_ref, q_ref, high_ref, p_ref, *refs):
    *piece_refs, g_near, e_near, q_near, sems, q_sem = refs
    replicas, rows, columns = g_ref.shape
    steps = rows // height
    copies = []
    for index in range(steps):
        at = (slice(None), pl.ds(index * height, height))
        copies.append([
            pltpu.make_async_copy(far.at[at], near.at[at], sems.at[which, index])
            for which, (far, near) in enumerate([(g_ref, g_near), (e_ref, e_near)])
        ])
        for copy in copies[-1]:
            copy.start()
        if index == 0:
            q_copy = pltpu.make_async_copy(q_ref, q_near, q_sem)
            q_copy.start()
    terms = []
    for index, pair in enumerate(copies):
        for copy in pair:
            copy.wait()
        row = pl.ds(index * height, height)
        for block in range(columns // LANES):
            at = pl.ds(block * LANES, LANES)
            total = (g_near[0, row, at] + e_near[0, row, at]).astype(F32)
            for replica in range(1, replicas):
                total = total + (g_near[replica, row, at] + e_near[replica, row, at]).astype(F32)
            high_ref[row, at] = (total * (1.0 / replicas)).astype(BF16)
        if index >= steps - 2:
            if index == steps - 2:
                q_copy.wait()
                row = pl.ds(0, rows - height)
            terms.append(dot(high_ref[row, :columns], q_near[...], ((1,), (1,))))
    p_ref[...] = fold(jnp.concatenate(terms, axis=0))
    high_ref[:, columns:] = jnp.zeros((rows, high_ref.shape[1] - columns), BF16)
    for flip, piece_ref in enumerate(piece_refs):
        width = piece_ref.shape[1]
        piece_ref[...] = high_ref[:, pl.ds(pl.multiple_of((x_ref[0] ^ flip) * width, LANES), width)]


def in_hbm(*values):
    return [pltpu.with_memory_space_constraint(value, pltpu.HBM) for value in values]


def start(place, gradient, error, q_turned, height=16):
    replicas, rows, columns = gradient.shape
    width = -(-columns // (X * LANES)) * LANES
    far = pl.BlockSpec(memory_space=pltpu.HBM)
    return pl.pallas_call(
        functools.partial(start_kernel, height),
        in_specs=[SMEM] + [far] * 3,
        out_specs=[VMEM] * (2 + X),
        out_shape=[
            jax.ShapeDtypeStruct((rows, X * width), BF16),
            jax.ShapeDtypeStruct((rows // 2, 2 * q_turned.shape[0]), F32),
        ]
        + [jax.ShapeDtypeStruct((rows, width), BF16)] * X,
        scratch_shapes=[
            pltpu.VMEM(gradient.shape, BF16),
            pltpu.VMEM(error.shape, BF16),
            pltpu.VMEM(q_turned.shape, BF16),
            pltpu.SemaphoreType.DMA((2, rows // height)),
            pltpu.SemaphoreType.DMA,
        ],
        compiler_params=params(24),
    )(place["x"], *in_hbm(gradient, error, q_turned))


def right_kernel(blocks, core_ref, own, one, two, three, high_ref, mine_ref, theirs_ref):
    p = unfold(total_of([own, one, two, three]))
    rank = p.shape[1]
    half = rank // 2
    first = core_ref[0] == 0
    turned = p.T
    stack = jnp.concatenate(split(turned, 3), axis=0)
    for block in range(blocks):
        at = pl.ds(block * LANES, LANES)
        top = dot(stack, high_ref[:, at])
        u = top[:rank] + (top[rank : 2 * rank] + top[2 * rank :])
        mine_ref[block] = jnp.where(first, u[:half], u[half:])
        theirs_ref[block] = jnp.where(first, u[half:], u[:half]).astype(BF16)
    gram = fold(dot(turned, p, ((1,), (0,)), HIGH))
    mine_ref[blocks] = gram
    for index, part in enumerate(split(gram, 3)):
        theirs_ref[blocks + index] = part


def right(place, parts, high, columns):
    rank = parts[0].shape[1] // 2
    blocks = columns // LANES
    return pl.pallas_call(
        functools.partial(right_kernel, blocks),
        in_specs=[SMEM] + [VMEM] * 5,
        out_specs=[VMEM] * 2,
        out_shape=[
            jax.ShapeDtypeStruct((blocks + 1, rank // 2, LANES), F32),
            jax.ShapeDtypeStruct((blocks + 3, rank // 2, LANES), BF16),
        ],
        compiler_params=params(24),
    )(place["core"], *parts, high)


def next_right_kernel(core_ref, x_ref, inverse_ref, *refs):
    *in_refs, mean_ref, mine_ref, theirs_ref, p_ref, all_ref = refs
    first = core_ref[0] == 0
    rank = inverse_ref.shape[0]
    t = total_of(in_refs)
    whole_blocks = t.shape[0] // rank
    t = [t[block * rank : (block + 1) * rank] for block in range(whole_blocks)] + [unfold(t[whole_blocks * rank :])]
    turned = dot(inverse_ref[...], jnp.concatenate(t, axis=1), ((1,), (0,)), HIGH)
    rank = turned.shape[0]
    half = rank // 2
    blocks = mine_ref.shape[0] - 1
    stack = jnp.concatenate(split(turned, 3), axis=0)
    for block in range(blocks):
        top = dot(stack, mean_ref[:, pl.ds(block * LANES, LANES)])
        u = top[:rank] + (top[rank : 2 * rank] + top[2 * rank :])
        mine_ref[block] = jnp.where(first, u[:half], u[half:])
        theirs_ref[block] = jnp.where(first, u[half:], u[:half])
    gram = fold(dot(turned, turned, ((1,), (1,)), HIGH))
    mine_ref[blocks] = gram
    theirs_ref[blocks] = gram
    all_ref[...] = turned.T
    rows = p_ref.shape[0]
    p_ref[...] = all_ref[pl.ds(pl.multiple_of(x_ref[0] * rows, rows), rows)]


def next_right(place, inverse, parts, mean):
    rows, width = mean.shape
    half = inverse.shape[0] // 2
    shape = jax.ShapeDtypeStruct((width // LANES + 1, half, LANES), F32)
    return pl.pallas_call(
        next_right_kernel,
        in_specs=[SMEM] * 2 + [VMEM] * (2 + Y),
        out_specs=[VMEM] * 3,
        out_shape=[shape, shape, jax.ShapeDtypeStruct((rows // X, 2 * half), F32)],
        scratch_shapes=[pltpu.VMEM((rows, 2 * half), F32)],
        compiler_params=params(24),
    )(place["core"], place["x"], inverse, *parts, mean)


def total_of(refs, *at):
    found = [ref[at] if at else ref[...] for ref in refs]
    if len(found) == 4:
        found = [found[0] + found[3], found[1] + found[2]]
    return found[0] + found[1]


def halve_kernel(near_ref, *refs):
    *in_refs, keep_ref, give_ref = refs
    rows = keep_ref.shape[1]
    place = near_ref[0] * rows
    keep_ref[...] = total_of(in_refs, slice(None), pl.ds(pl.multiple_of(place, rows), rows))
    give_ref[...] = total_of(in_refs, slice(None), pl.ds(pl.multiple_of(rows - place, rows), rows))


def sum_kernel(*refs):
    refs[-1][...] = total_of(refs[:-1])


def join_kernel(near_ref, here_ref, there_ref, chunk_ref, gram_ref):
    per, rows = chunk_ref.shape[0], here_ref.shape[1]
    place = near_ref[0] * rows
    chunk_ref[:, pl.ds(pl.multiple_of(place, rows), rows)] = here_ref[:per]
    chunk_ref[:, pl.ds(pl.multiple_of(rows - place, rows), rows)] = there_ref[:per]
    first = near_ref[0] == 0
    here, there = here_ref[per], there_ref[per]
    packed = jnp.concatenate([jnp.where(first, here, there), jnp.where(first, there, here)], axis=0)
    half, rank = packed.shape[0], gram_ref.shape[0]
    gram_ref[:half] = packed[:, :rank]
    gram_ref[half:] = packed[:, rank:]


def small(kernel, operands, shapes, scalars=0, kind=F32, scratch=()):
    return pl.pallas_call(
        kernel,
        in_specs=[SMEM] * scalars + [VMEM] * (len(operands) - scalars),
        out_specs=[VMEM] * len(shapes),
        out_shape=[jax.ShapeDtypeStruct(shape, kind) for shape in shapes],
        scratch_shapes=scratch,
        compiler_params=params(8),
    )(*operands)


def pack(ref, u, gram):
    per = u.shape[0]
    ref[:per] = u.astype(BF16)
    parts = [part.astype(F32) for part in split(gram, 3)]
    spare = ref.shape[1] - 3 * gram.shape[0]
    ref[per] = jnp.concatenate(parts + [jnp.zeros((spare, LANES), F32)], axis=0).astype(BF16)


def unpack(ref):
    per, rows, _ = ref.shape
    block = ref[per - 1].astype(F32)
    part = rows // X
    return ref[: per - 1].astype(F32), block[:part] + (block[part : 2 * part] + block[2 * part : 3 * part])


def cut_coarse_kernel(x_ref, a_ref, b_ref, *refs):
    *out_refs, gram_ref = refs
    last = a_ref.shape[0] - 1
    per = out_refs[0].shape[0] - 1
    part = gram_ref.shape[0] // X
    gram = b_ref[last].astype(F32) + (b_ref[last + 1].astype(F32) + b_ref[last + 2].astype(F32))
    gram_ref[...] = a_ref[last] + gram
    for flip, out_ref in enumerate(out_refs):
        owner = x_ref[0] ^ flip
        at = pl.ds(owner * per, per)
        rows = pl.ds(pl.multiple_of(owner * part, part), part)
        pack(out_ref, a_ref[at] + b_ref[at].astype(F32), gram_ref[rows])


def sum_coarse_kernel(*refs):
    found = [unpack(ref) for ref in refs[:-1]]
    if len(found) == 4:
        found = [[a + b for a, b in zip(found[k], found[3 - k])] for k in range(2)]
    pack(refs[-1], *[a + b for a, b in zip(*found)])


def coarse_sum(place, mine, theirs):
    per, (rows, lanes) = mine.shape[0] // X, mine.shape[1:]
    shape = (per + 1, rows, lanes)
    scratch = [pltpu.VMEM((rows, lanes), F32)]
    cuts = small(cut_coarse_kernel, (place["x"], mine, swap(theirs, "core")), [shape] * X, 1, BF16, scratch)
    (part,) = small(sum_coarse_kernel, around(cuts, "x"), [shape], 0, BF16)
    (part,) = small(sum_coarse_kernel, (part, swap(part, "near")), [shape], 0, BF16)
    (part,) = small(sum_coarse_kernel, around(part, "far"), [shape], 0, BF16)
    return part


def around(value, axis):
    if isinstance(value, (list, tuple)):
        return [value[0]] + [flipped(value[flip], axis, flip) for flip in SENT[1:]]
    return [value] + [flipped(value, axis, flip) for flip in SHARED[1:]]


def flipped(value, axis, flip):
    return lax.ppermute(value, axis, [(i, i ^ flip) for i in range(4)])


def swap(value, axis):
    return lax.ppermute(value, axis, [(0, 1), (1, 0)])


def all_sum(place, mine, theirs, gradient, error):
    blocks, rows, lanes = mine.shape
    half = (blocks, rows // 2, lanes)
    keep, give = small(halve_kernel, (place["near"], mine, swap(theirs, "core")), [half] * 2, 1)
    (both,) = small(sum_kernel, (keep, swap(give, "near")), [half])
    (total,) = small(sum_kernel, around(both, "far"), [half])
    rank = 2 * rows
    chunk, gram = small(
        join_kernel, (place["near"], total, swap(total, "near")), [(blocks - 1, rows, lanes), (rank, rank)], 1
    )
    ready = inverse_and_fetch(gram, gradient, error)
    here = around(chunk, "x")
    first = swap(here[0], "core")
    *ready, here[1], here[2], here[3] = lax.optimization_barrier([*ready, *here[1:]])
    return here, [first] + [swap(part, "core") for part in here[1:]], ready


def whole(first, a, b):
    return jnp.concatenate([jnp.where(first, a, b), jnp.where(first, b, a)], axis=0)


def gather(core_ref, x_ref, refs, u_ref, per):
    first = core_ref[0] == 0
    parts = u_ref.shape[0] // (2 * refs[0].shape[1])
    for flip, a_ref, b_ref in zip(SHARED, refs[:X], refs[X:]):
        owner = x_ref[0] ^ flip
        for index in range(per):
            at = pl.ds(pl.multiple_of((owner * per + index) * LANES, LANES), LANES)
            u = whole(first, a_ref[index].astype(F32), b_ref[index].astype(F32))
            u_ref[:, at] = jnp.concatenate(split(u, parts), axis=0)


def left_kernel(core_ref, x_ref, part_ref, other_ref, *refs):
    *piece_refs, mean_ref, out_ref = refs
    height = piece_refs[0].shape[0]
    for flip, piece_ref in zip(SENT, piece_refs):
        mean_ref[pl.ds(pl.multiple_of((x_ref[0] ^ flip) * height, height), height)] = piece_ref[...]
    per = part_ref.shape[0] - 1
    first = core_ref[0] == 0
    u = jnp.concatenate([whole(first, part_ref[block], other_ref[block]) for block in range(per)], axis=1)
    rows = mean_ref.shape[0]
    out_ref[:, :rows] = dot(u, mean_ref[...], ((1,), (1,)))
    quarter = unpack(part_ref)[1]
    side = quarter.shape[1] // 2
    quarter = jnp.concatenate([quarter[:, :side], quarter[:, side:]], axis=0)
    spare = out_ref.shape[0] - quarter.shape[0]
    out_ref[:, rows:] = jnp.concatenate([quarter, jnp.zeros((spare, side), F32)], axis=0)


def left(place, part, pieces):
    height, width = pieces[0].shape
    rows = X * height
    half, lanes = part.shape[1:]
    return pl.pallas_call(
        left_kernel,
        in_specs=[SMEM] * 2 + [VMEM] * (2 + X),
        out_specs=[VMEM] * 2,
        out_shape=[
            jax.ShapeDtypeStruct((rows, width), BF16),
            jax.ShapeDtypeStruct((2 * half, rows + lanes // 2), F32),
        ],
        compiler_params=params(24),
    )(place["core"], place["x"], part, swap(part, "core"), *pieces)


def left_sum_kernel(x_ref, *refs):
    *in_refs, t_ref, gram_ref = refs
    rank = gram_ref.shape[0]
    half = rank // 2
    rows = in_refs[0].shape[1] - rank
    t = total_of(in_refs, slice(None), slice(0, rows))
    whole_blocks = rows // LANES
    for block in range(whole_blocks):
        t_ref[block * rank : (block + 1) * rank] = t[:, block * LANES : (block + 1) * LANES]
    t_ref[whole_blocks * rank :] = fold(t[:, whole_blocks * LANES :])
    part = half // X
    for flip, in_ref in zip(SHARED, in_refs):
        quarter = in_ref[: 2 * part, rows:]
        place = (x_ref[0] ^ flip) * part
        gram_ref[pl.ds(pl.multiple_of(place, part), part)] = quarter[:part]
        gram_ref[pl.ds(pl.multiple_of(half + place, part), part)] = quarter[part:]


def lower_inverse(gram):
    rank = gram.shape[0]
    at_row = lax.broadcasted_iota(jnp.int32, (rank, rank), 0)
    at_col = lax.broadcasted_iota(jnp.int32, (rank, rank), 1)
    diagonal = jnp.where(at_row == at_col, gram, 0.0)
    down = lax.rsqrt(jnp.sum(diagonal, axis=1, keepdims=True))
    across = lax.rsqrt(jnp.sum(diagonal, axis=0, keepdims=True))
    work = jnp.concatenate([gram * down * across, jnp.where(at_row == at_col, across, 0.0)], axis=1)
    done = []
    for step in range(0, rank, 2):
        low = step // 8 * 8
        at = step - low
        work = work[at // 8 * 8 :] if at else (work[8:] if step else work)
        one = jnp.broadcast_to(work[:, step : step + 1], work.shape)
        two = jnp.broadcast_to(work[:, step + 1 : step + 2], work.shape)
        first, second = work[at : at + 1], work[at + 1 : at + 2]
        a, b, c = one[at : at + 1], one[at + 1 : at + 2], two[at + 1 : at + 2]
        det = a * c - b * b
        left_over = a * second - b * first
        inverse = 1.0 / det
        done.append((first * lax.rsqrt(a))[:, rank:])
        done.append((left_over * lax.rsqrt(a * det))[:, rank:])
        work = work - (one * ((c * first - b * second) * inverse) + two * (left_over * inverse))
    return jnp.concatenate(done, axis=0)


def inverse_kernel(gram_ref, out_ref):
    out_ref[...] = lower_inverse(gram_ref[...])


def inverse_of(gram):
    return pl.pallas_call(
        inverse_kernel,
        in_specs=[VMEM],
        out_specs=VMEM,
        out_shape=jax.ShapeDtypeStruct(gram.shape, F32),
        compiler_params=params(4),
        cost_estimate=pl.CostEstimate(flops=10_000_000, bytes_accessed=5_000_000, transcendentals=0),
    )(gram)


def fetch_kernel(gram_ref, g_ref, e_ref, out_ref, g_near, e_near, sems):
    copies = [
        pltpu.make_async_copy(far, near, sems.at[index])
        for index, (far, near) in enumerate([(g_ref, g_near), (e_ref, e_near)])
    ]
    for copy in copies:
        copy.start()
    out_ref[...] = lower_inverse(gram_ref[...])
    for copy in copies:
        copy.wait()


def inverse_and_fetch(gram, gradient, error):
    far = pl.BlockSpec(memory_space=pltpu.HBM)
    return pl.pallas_call(
        fetch_kernel,
        in_specs=[VMEM, far, far],
        out_specs=[VMEM] * 3,
        out_shape=[
            jax.ShapeDtypeStruct(gram.shape, F32),
            pltpu.VMEM(gradient.shape, BF16),
            pltpu.VMEM(error.shape, BF16),
        ],
        scratch_shapes=[pltpu.SemaphoreType.DMA((2,))],
        compiler_params=params(24),
        cost_estimate=pl.CostEstimate(flops=10_000_000, bytes_accessed=5_000_000, transcendentals=0),
    )(gram, *in_hbm(gradient, error))


def end_kernel(core_ref, x_ref, *refs):
    *refs, inverse_ref, p_ref, g_ref, e_ref, new_ref, q_ref, u_ref, half_ref = refs
    rank = p_ref.shape[1]
    width = q_ref.shape[1]
    step = pl.program_id(0)

    @pl.when(step == 0)
    def _():
        gather(core_ref, x_ref, refs, u_ref, refs[0].shape[0])
        half_ref[...] = dot(p_ref[...], inverse_ref[...], ((1,), (1,)), HIGH).astype(BF16)

    at = pl.ds(pl.multiple_of(step * width, LANES), width)
    high, mid, low = split(inverse_ref[...], 3)
    q = dot(low, u_ref[:rank, at]) + dot(jnp.concatenate([mid] * 2, axis=1), u_ref[: 2 * rank, at])
    q = dot(jnp.concatenate([high] * 3, axis=1), u_ref[:, at]) + q
    q_ref[...] = q
    for block in range(width // LANES):
        recon = dot(half_ref[...], q[:, block * LANES : (block + 1) * LANES].astype(BF16))
        part = pl.ds(block * LANES, LANES)
        far = pl.ds(pl.multiple_of(step * width + block * LANES, LANES), LANES)
        for replica in range(g_ref.shape[0]):
            corrected = g_ref[replica, :, far] + e_ref[replica, :, far]
            new_ref[replica, :, part] = (corrected.astype(F32) - recon).astype(BF16)


def end(place, here, there, p, inverse, gradient, error, width=1152):
    replicas, rows, columns = gradient.shape
    rank = p.shape[1]
    per = here[0].shape[0]
    wide = pl.BlockSpec((replicas, rows, width), lambda j: (0, 0, j))
    return pl.pallas_call(
        end_kernel,
        grid=(columns // width,),
        in_specs=[SMEM] * 2 + [VMEM] * (2 * X + 4),
        out_specs=[wide, pl.BlockSpec((rank, width), lambda j: (0, j))],
        out_shape=[
            jax.ShapeDtypeStruct(gradient.shape, BF16),
            jax.ShapeDtypeStruct((rank, columns), F32),
        ],
        scratch_shapes=[pltpu.VMEM((3 * rank, X * per * LANES), BF16), pltpu.VMEM((rows, rank), BF16)],
        compiler_params=params(24),
    )(place["core"], place["x"], *here, *there, inverse, p, gradient, error)


def per_device(gradient, error_buffer, q_start):
    place = {axis: lax.axis_index(axis).astype(jnp.int32).reshape(1) for axis in ("x", "near", "core")}
    high, term, *pieces = start(place, gradient, error_buffer, q_start.T)
    parts = around(term, "y")
    pieces = around(pieces, "x")
    part = coarse_sum(place, *right(place, parts, high, gradient.shape[2]))
    mean, term = left(place, part, pieces)
    rank, width = term.shape
    term, gram = small(
        left_sum_kernel, (place["x"], *around(term, "x")), [(rank * (width - rank) // LANES, LANES), (rank, rank)], 1
    )
    mine, theirs, p = next_right(place, inverse_of(gram), around(term, "y"), mean)
    here, there, ready = all_sum(place, mine, theirs, gradient, error_buffer)
    new_error, q_factor = end(place, here, there, p, *ready)
    return new_error, q_factor.T


def solution(mesh):
    fine = Mesh(mesh.devices.reshape(X, FAR, NEAR, CORES, Y), ("x", "far", "near", "core", "y"))
    rows = ("x", "far", "near", "core")
    return jax.shard_map(
        per_device,
        mesh=fine,
        in_specs=(P(None, rows, "y"), P(None, rows, "y"), P("y", None)),
        out_specs=(P(None, rows, "y"), P("y", None)),
        check_vma=False,
    )
```

```python
import functools

import jax
import jax.numpy as jnp
from jax import lax
from jax.experimental import pallas as pl
from jax.experimental.pallas import tpu as pltpu
from jax.sharding import Mesh
from jax.sharding import PartitionSpec as P

X, FAR, NEAR, CORES, Y = 4, 4, 2, 2, 4
LANES = 128
SENT, SHARED = (0, 2, 1, 3), (0, 1, 3, 2)
F32, BF16 = jnp.float32, jnp.bfloat16
HIGH = lax.Precision.HIGHEST
VMEM = pl.BlockSpec(memory_space=pltpu.VMEM)
SMEM = pl.BlockSpec(memory_space=pltpu.SMEM)


def split(value, parts):
    found = []
    for _ in range(parts):
        found.append(value.astype(BF16))
        value = value - found[-1].astype(F32)
    return found


def dot(a, b, contract=((1,), (0,)), precision=None):
    return lax.dot_general(a, b, (contract, ((), ())), precision=precision, preferred_element_type=F32)


def fold(value):
    half = value.shape[0] // 2
    return jnp.concatenate([value[:half], value[half:]], axis=1)


def unfold(value):
    half = value.shape[1] // 2
    return jnp.concatenate([value[:, :half], value[:, half:]], axis=0)


def params(mib, **more):
    return pltpu.CompilerParams(vmem_limit_bytes=mib << 20, **more)


def start_kernel(height, x_ref, g_ref, e_ref, q_ref, high_ref, p_ref, *refs):
    *piece_refs, g_near, e_near, q_near, sems, q_sem = refs
    replicas, rows, columns = g_ref.shape
    steps = rows // height
    copies = []
    for index in range(steps):
        at = (slice(None), pl.ds(index * height, height))
        copies.append([
            pltpu.make_async_copy(far.at[at], near.at[at], sems.at[which, index])
            for which, (far, near) in enumerate([(g_ref, g_near), (e_ref, e_near)])
        ])
        for copy in copies[-1]:
            copy.start()
        if index == 0:
            q_copy = pltpu.make_async_copy(q_ref, q_near, q_sem)
            q_copy.start()
    terms = []
    for index, pair in enumerate(copies):
        for copy in pair:
            copy.wait()
        row = pl.ds(index * height, height)
        for block in range(columns // LANES):
            at = pl.ds(block * LANES, LANES)
            total = (g_near[0, row, at] + e_near[0, row, at]).astype(F32)
            for replica in range(1, replicas):
                total = total + (g_near[replica, row, at] + e_near[replica, row, at]).astype(F32)
            high_ref[row, at] = (total * (1.0 / replicas)).astype(BF16)
        if index >= steps - 2:
            if index == steps - 2:
                q_copy.wait()
                row = pl.ds(0, rows - height)
            terms.append(dot(high_ref[row, :columns], q_near[...], ((1,), (1,))))
    p_ref[...] = fold(jnp.concatenate(terms, axis=0))
    high_ref[:, columns:] = jnp.zeros((rows, high_ref.shape[1] - columns), BF16)
    for flip, piece_ref in enumerate(piece_refs):
        width = piece_ref.shape[1]
        piece_ref[...] = high_ref[:, pl.ds(pl.multiple_of((x_ref[0] ^ flip) * width, LANES), width)]


def in_hbm(*values):
    return [pltpu.with_memory_space_constraint(value, pltpu.HBM) for value in values]


def start(place, gradient, error, q_turned, height=16):
    replicas, rows, columns = gradient.shape
    width = -(-columns // (X * LANES)) * LANES
    far = pl.BlockSpec(memory_space=pltpu.HBM)
    return pl.pallas_call(
        functools.partial(start_kernel, height),
        in_specs=[SMEM] + [far] * 3,
        out_specs=[VMEM] * (2 + X),
        out_shape=[
            jax.ShapeDtypeStruct((rows, X * width), BF16),
            jax.ShapeDtypeStruct((rows // 2, 2 * q_turned.shape[0]), F32),
        ]
        + [jax.ShapeDtypeStruct((rows, width), BF16)] * X,
        scratch_shapes=[
            pltpu.VMEM(gradient.shape, BF16),
            pltpu.VMEM(error.shape, BF16),
            pltpu.VMEM(q_turned.shape, BF16),
            pltpu.SemaphoreType.DMA((2, rows // height)),
            pltpu.SemaphoreType.DMA,
        ],
        compiler_params=params(24),
    )(place["x"], *in_hbm(gradient, error, q_turned))


def right_kernel(blocks, core_ref, own, one, two, three, high_ref, mine_ref, theirs_ref):
    p = unfold(total_of([own, one, two, three]))
    rank = p.shape[1]
    half = rank // 2
    first = core_ref[0] == 0
    turned = p.T
    stack = jnp.concatenate(split(turned, 3), axis=0)
    for block in range(blocks):
        at = pl.ds(block * LANES, LANES)
        top = dot(stack, high_ref[:, at])
        u = top[:rank] + (top[rank : 2 * rank] + top[2 * rank :])
        mine_ref[block] = jnp.where(first, u[:half], u[half:])
        theirs_ref[block] = jnp.where(first, u[half:], u[:half]).astype(BF16)
    gram = fold(dot(turned, p, ((1,), (0,)), HIGH))
    mine_ref[blocks] = gram
    for index, part in enumerate(split(gram, 3)):
        theirs_ref[blocks + index] = part


def right(place, parts, high, columns):
    rank = parts[0].shape[1] // 2
    blocks = columns // LANES
    return pl.pallas_call(
        functools.partial(right_kernel, blocks),
        in_specs=[SMEM] + [VMEM] * 5,
        out_specs=[VMEM] * 2,
        out_shape=[
            jax.ShapeDtypeStruct((blocks + 1, rank // 2, LANES), F32),
            jax.ShapeDtypeStruct((blocks + 3, rank // 2, LANES), BF16),
        ],
        compiler_params=params(24),
    )(place["core"], *parts, high)


def next_right_kernel(core_ref, x_ref, inverse_ref, *refs):
    *in_refs, mean_ref, mine_ref, theirs_ref, p_ref, all_ref = refs
    first = core_ref[0] == 0
    rank = inverse_ref.shape[0]
    t = total_of(in_refs)
    whole_blocks = t.shape[0] // rank
    t = [t[block * rank : (block + 1) * rank] for block in range(whole_blocks)] + [unfold(t[whole_blocks * rank :])]
    turned = dot(inverse_ref[...], jnp.concatenate(t, axis=1), ((1,), (0,)), HIGH)
    rank = turned.shape[0]
    half = rank // 2
    blocks = mine_ref.shape[0] - 1
    stack = jnp.concatenate(split(turned, 3), axis=0)
    for block in range(blocks):
        top = dot(stack, mean_ref[:, pl.ds(block * LANES, LANES)])
        u = top[:rank] + (top[rank : 2 * rank] + top[2 * rank :])
        mine_ref[block] = jnp.where(first, u[:half], u[half:])
        theirs_ref[block] = jnp.where(first, u[half:], u[:half])
    gram = fold(dot(turned, turned, ((1,), (1,)), HIGH))
    mine_ref[blocks] = gram
    theirs_ref[blocks] = gram
    all_ref[...] = turned.T
    rows = p_ref.shape[0]
    p_ref[...] = all_ref[pl.ds(pl.multiple_of(x_ref[0] * rows, rows), rows)]


def next_right(place, inverse, parts, mean):
    rows, width = mean.shape
    half = inverse.shape[0] // 2
    shape = jax.ShapeDtypeStruct((width // LANES + 1, half, LANES), F32)
    return pl.pallas_call(
        next_right_kernel,
        in_specs=[SMEM] * 2 + [VMEM] * (2 + Y),
        out_specs=[VMEM] * 3,
        out_shape=[shape, shape, jax.ShapeDtypeStruct((rows // X, 2 * half), F32)],
        scratch_shapes=[pltpu.VMEM((rows, 2 * half), F32)],
        compiler_params=params(24),
    )(place["core"], place["x"], inverse, *parts, mean)


def total_of(refs, *at):
    found = [ref[at] if at else ref[...] for ref in refs]
    if len(found) == 4:
        found = [found[0] + found[3], found[1] + found[2]]
    return found[0] + found[1]


def halve_kernel(near_ref, *refs):
    *in_refs, keep_ref, give_ref = refs
    rows = keep_ref.shape[1]
    place = near_ref[0] * rows
    keep_ref[...] = total_of(in_refs, slice(None), pl.ds(pl.multiple_of(place, rows), rows))
    give_ref[...] = total_of(in_refs, slice(None), pl.ds(pl.multiple_of(rows - place, rows), rows))


def sum_kernel(*refs):
    refs[-1][...] = total_of(refs[:-1])


def join_kernel(near_ref, here_ref, there_ref, chunk_ref, gram_ref):
    per, rows = chunk_ref.shape[0], here_ref.shape[1]
    place = near_ref[0] * rows
    chunk_ref[:, pl.ds(pl.multiple_of(place, rows), rows)] = here_ref[:per]
    chunk_ref[:, pl.ds(pl.multiple_of(rows - place, rows), rows)] = there_ref[:per]
    first = near_ref[0] == 0
    here, there = here_ref[per], there_ref[per]
    packed = jnp.concatenate([jnp.where(first, here, there), jnp.where(first, there, here)], axis=0)
    half, rank = packed.shape[0], gram_ref.shape[0]
    gram_ref[:half] = packed[:, :rank]
    gram_ref[half:] = packed[:, rank:]


def small(kernel, operands, shapes, scalars=0, kind=F32, scratch=()):
    return pl.pallas_call(
        kernel,
        in_specs=[SMEM] * scalars + [VMEM] * (len(operands) - scalars),
        out_specs=[VMEM] * len(shapes),
        out_shape=[jax.ShapeDtypeStruct(shape, kind) for shape in shapes],
        scratch_shapes=scratch,
        compiler_params=params(8),
    )(*operands)


def pack(ref, u, gram):
    per = u.shape[0]
    ref[:per] = u.astype(BF16)
    parts = [part.astype(F32) for part in split(gram, 3)]
    spare = ref.shape[1] - 3 * gram.shape[0]
    ref[per] = jnp.concatenate(parts + [jnp.zeros((spare, LANES), F32)], axis=0).astype(BF16)


def unpack(ref):
    per, rows, _ = ref.shape
    block = ref[per - 1].astype(F32)
    part = rows // X
    return ref[: per - 1].astype(F32), block[:part] + (block[part : 2 * part] + block[2 * part : 3 * part])


def cut_coarse_kernel(x_ref, a_ref, b_ref, *refs):
    *out_refs, gram_ref = refs
    last = a_ref.shape[0] - 1
    per = out_refs[0].shape[0] - 1
    part = gram_ref.shape[0] // X
    gram = b_ref[last].astype(F32) + (b_ref[last + 1].astype(F32) + b_ref[last + 2].astype(F32))
    gram_ref[...] = a_ref[last] + gram
    for flip, out_ref in enumerate(out_refs):
        owner = x_ref[0] ^ flip
        at = pl.ds(owner * per, per)
        rows = pl.ds(pl.multiple_of(owner * part, part), part)
        pack(out_ref, a_ref[at] + b_ref[at].astype(F32), gram_ref[rows])


def sum_coarse_kernel(*refs):
    found = [unpack(ref) for ref in refs[:-1]]
    if len(found) == 4:
        found = [[a + b for a, b in zip(found[k], found[3 - k])] for k in range(2)]
    pack(refs[-1], *[a + b for a, b in zip(*found)])


def coarse_sum(place, mine, theirs):
    per, (rows, lanes) = mine.shape[0] // X, mine.shape[1:]
    shape = (per + 1, rows, lanes)
    scratch = [pltpu.VMEM((rows, lanes), F32)]
    cuts = small(cut_coarse_kernel, (place["x"], mine, swap(theirs, "core")), [shape] * X, 1, BF16, scratch)
    (part,) = small(sum_coarse_kernel, around(cuts, "x"), [shape], 0, BF16)
    (part,) = small(sum_coarse_kernel, (part, swap(part, "near")), [shape], 0, BF16)
    (part,) = small(sum_coarse_kernel, around(part, "far"), [shape], 0, BF16)
    return part


def around(value, axis):
    if isinstance(value, (list, tuple)):
        return [value[0]] + [flipped(value[flip], axis, flip) for flip in SENT[1:]]
    return [value] + [flipped(value, axis, flip) for flip in SHARED[1:]]


def flipped(value, axis, flip):
    return lax.ppermute(value, axis, [(i, i ^ flip) for i in range(4)])


def swap(value, axis):
    return lax.ppermute(value, axis, [(0, 1), (1, 0)])


def all_sum(place, mine, theirs, gradient, error):
    blocks, rows, lanes = mine.shape
    half = (blocks, rows // 2, lanes)
    keep, give = small(halve_kernel, (place["near"], mine, swap(theirs, "core")), [half] * 2, 1)
    (both,) = small(sum_kernel, (keep, swap(give, "near")), [half])
    (total,) = small(sum_kernel, around(both, "far"), [half])
    rank = 2 * rows
    chunk, gram = small(
        join_kernel, (place["near"], total, swap(total, "near")), [(blocks - 1, rows, lanes), (rank, rank)], 1
    )
    ready = inverse_and_fetch(gram, gradient, error)
    here = around(chunk, "x")
    first = swap(here[0], "core")
    *ready, here[1], here[2], here[3] = lax.optimization_barrier([*ready, *here[1:]])
    return here, [first] + [swap(part, "core") for part in here[1:]], ready


def whole(first, a, b):
    return jnp.concatenate([jnp.where(first, a, b), jnp.where(first, b, a)], axis=0)


def gather(core_ref, x_ref, refs, u_ref, per):
    first = core_ref[0] == 0
    parts = u_ref.shape[0] // (2 * refs[0].shape[1])
    for flip, a_ref, b_ref in zip(SHARED, refs[:X], refs[X:]):
        owner = x_ref[0] ^ flip
        for index in range(per):
            at = pl.ds(pl.multiple_of((owner * per + index) * LANES, LANES), LANES)
            u = whole(first, a_ref[index].astype(F32), b_ref[index].astype(F32))
            u_ref[:, at] = jnp.concatenate(split(u, parts), axis=0)


def left_kernel(core_ref, x_ref, part_ref, other_ref, *refs):
    *piece_refs, mean_ref, out_ref = refs
    height = piece_refs[0].shape[0]
    for flip, piece_ref in zip(SENT, piece_refs):
        mean_ref[pl.ds(pl.multiple_of((x_ref[0] ^ flip) * height, height), height)] = piece_ref[...]
    per = part_ref.shape[0] - 1
    first = core_ref[0] == 0
    u = jnp.concatenate([whole(first, part_ref[block], other_ref[block]) for block in range(per)], axis=1)
    rows = mean_ref.shape[0]
    out_ref[:, :rows] = dot(u, mean_ref[...], ((1,), (1,)))
    quarter = unpack(part_ref)[1]
    side = quarter.shape[1] // 2
    quarter = jnp.concatenate([quarter[:, :side], quarter[:, side:]], axis=0)
    spare = out_ref.shape[0] - quarter.shape[0]
    out_ref[:, rows:] = jnp.concatenate([quarter, jnp.zeros((spare, side), F32)], axis=0)


def left(place, part, pieces):
    height, width = pieces[0].shape
    rows = X * height
    half, lanes = part.shape[1:]
    return pl.pallas_call(
        left_kernel,
        in_specs=[SMEM] * 2 + [VMEM] * (2 + X),
        out_specs=[VMEM] * 2,
        out_shape=[
            jax.ShapeDtypeStruct((rows, width), BF16),
            jax.ShapeDtypeStruct((2 * half, rows + lanes // 2), F32),
        ],
        compiler_params=params(24),
    )(place["core"], place["x"], part, swap(part, "core"), *pieces)


def left_sum_kernel(x_ref, *refs):
    *in_refs, t_ref, gram_ref = refs
    rank = gram_ref.shape[0]
    half = rank // 2
    rows = in_refs[0].shape[1] - rank
    t = total_of(in_refs, slice(None), slice(0, rows))
    whole_blocks = rows // LANES
    for block in range(whole_blocks):
        t_ref[block * rank : (block + 1) * rank] = t[:, block * LANES : (block + 1) * LANES]
    t_ref[whole_blocks * rank :] = fold(t[:, whole_blocks * LANES :])
    part = half // X
    for flip, in_ref in zip(SHARED, in_refs):
        quarter = in_ref[: 2 * part, rows:]
        place = (x_ref[0] ^ flip) * part
        gram_ref[pl.ds(pl.multiple_of(place, part), part)] = quarter[:part]
        gram_ref[pl.ds(pl.multiple_of(half + place, part), part)] = quarter[part:]


def lower_inverse(gram):
    rank = gram.shape[0]
    at_row = lax.broadcasted_iota(jnp.int32, (rank, rank), 0)
    at_col = lax.broadcasted_iota(jnp.int32, (rank, rank), 1)
    diagonal = jnp.where(at_row == at_col, gram, 0.0)
    down = lax.rsqrt(jnp.sum(diagonal, axis=1, keepdims=True))
    across = lax.rsqrt(jnp.sum(diagonal, axis=0, keepdims=True))
    work = jnp.concatenate([gram * down * across, jnp.where(at_row == at_col, across, 0.0)], axis=1)
    done = []
    for step in range(0, rank, 2):
        low = step // 8 * 8
        at = step - low
        work = work[at // 8 * 8 :] if at else (work[8:] if step else work)
        one = jnp.broadcast_to(work[:, step : step + 1], work.shape)
        two = jnp.broadcast_to(work[:, step + 1 : step + 2], work.shape)
        first, second = work[at : at + 1], work[at + 1 : at + 2]
        a, b, c = one[at : at + 1], one[at + 1 : at + 2], two[at + 1 : at + 2]
        det = a * c - b * b
        left_over = a * second - b * first
        inverse = 1.0 / det
        done.append((first * lax.rsqrt(a))[:, rank:])
        done.append((left_over * lax.rsqrt(a * det))[:, rank:])
        work = work - (one * ((c * first - b * second) * inverse) + two * (left_over * inverse))
    return jnp.concatenate(done, axis=0)


def inverse_kernel(gram_ref, out_ref):
    out_ref[...] = lower_inverse(gram_ref[...])


def inverse_of(gram):
    return pl.pallas_call(
        inverse_kernel,
        in_specs=[VMEM],
        out_specs=VMEM,
        out_shape=jax.ShapeDtypeStruct(gram.shape, F32),
        compiler_params=params(4),
        cost_estimate=pl.CostEstimate(flops=10_000_000, bytes_accessed=5_000_000, transcendentals=0),
    )(gram)


def fetch_kernel(gram_ref, g_ref, e_ref, out_ref, g_near, e_near, sems):
    copies = [
        pltpu.make_async_copy(far, near, sems.at[index])
        for index, (far, near) in enumerate([(g_ref, g_near), (e_ref, e_near)])
    ]
    for copy in copies:
        copy.start()
    out_ref[...] = lower_inverse(gram_ref[...])
    for copy in copies:
        copy.wait()


def inverse_and_fetch(gram, gradient, error):
    far = pl.BlockSpec(memory_space=pltpu.HBM)
    return pl.pallas_call(
        fetch_kernel,
        in_specs=[VMEM, far, far],
        out_specs=[VMEM] * 3,
        out_shape=[
            jax.ShapeDtypeStruct(gram.shape, F32),
            pltpu.VMEM(gradient.shape, BF16),
            pltpu.VMEM(error.shape, BF16),
        ],
        scratch_shapes=[pltpu.SemaphoreType.DMA((2,))],
        compiler_params=params(24),
        cost_estimate=pl.CostEstimate(flops=10_000_000, bytes_accessed=5_000_000, transcendentals=0),
    )(gram, *in_hbm(gradient, error))


def end_kernel(core_ref, x_ref, *refs):
    *refs, inverse_ref, p_ref, g_ref, e_ref, new_ref, q_ref, u_ref, half_ref = refs
    rank = p_ref.shape[1]
    width = q_ref.shape[1]
    step = pl.program_id(0)

    @pl.when(step == 0)
    def _():
        gather(core_ref, x_ref, refs, u_ref, refs[0].shape[0])
        half_ref[...] = dot(p_ref[...], inverse_ref[...], ((1,), (1,)), HIGH).astype(BF16)

    at = pl.ds(pl.multiple_of(step * width, LANES), width)
    high, mid, low = split(inverse_ref[...], 3)
    q = dot(low, u_ref[:rank, at]) + dot(jnp.concatenate([mid] * 2, axis=1), u_ref[: 2 * rank, at])
    q = dot(jnp.concatenate([high] * 3, axis=1), u_ref[:, at]) + q
    q_ref[...] = q
    for block in range(width // LANES):
        recon = dot(half_ref[...], q[:, block * LANES : (block + 1) * LANES].astype(BF16))
        part = pl.ds(block * LANES, LANES)
        far = pl.ds(pl.multiple_of(step * width + block * LANES, LANES), LANES)
        for replica in range(g_ref.shape[0]):
            corrected = g_ref[replica, :, far] + e_ref[replica, :, far]
            new_ref[replica, :, part] = (corrected.astype(F32) - recon).astype(BF16)


def end(place, here, there, p, inverse, gradient, error, width=384):
    replicas, rows, columns = gradient.shape
    rank = p.shape[1]
    per = here[0].shape[0]
    wide = pl.BlockSpec((replicas, rows, width), lambda j: (0, 0, j))
    return pl.pallas_call(
        end_kernel,
        grid=(columns // width,),
        in_specs=[SMEM] * 2 + [VMEM] * (2 * X + 4),
        out_specs=[wide, pl.BlockSpec((rank, width), lambda j: (0, j))],
        out_shape=[
            jax.ShapeDtypeStruct(gradient.shape, BF16),
            jax.ShapeDtypeStruct((rank, columns), F32),
        ],
        scratch_shapes=[pltpu.VMEM((3 * rank, X * per * LANES), BF16), pltpu.VMEM((rows, rank), BF16)],
        compiler_params=params(24),
    )(place["core"], place["x"], *here, *there, inverse, p, gradient, error)


def per_device(gradient, error_buffer, q_start):
    place = {axis: lax.axis_index(axis).astype(jnp.int32).reshape(1) for axis in ("x", "near", "core")}
    high, term, *pieces = start(place, gradient, error_buffer, q_start.T)
    parts = around(term, "y")
    pieces = around(pieces, "x")
    part = coarse_sum(place, *right(place, parts, high, gradient.shape[2]))
    mean, term = left(place, part, pieces)
    rank, width = term.shape
    term, gram = small(
        left_sum_kernel, (place["x"], *around(term, "x")), [(rank * (width - rank) // LANES, LANES), (rank, rank)], 1
    )
    mine, theirs, p = next_right(place, inverse_of(gram), around(term, "y"), mean)
    here, there, ready = all_sum(place, mine, theirs, gradient, error_buffer)
    new_error, q_factor = end(place, here, there, p, *ready)
    return new_error, q_factor.T


def solution(mesh):
    fine = Mesh(mesh.devices.reshape(X, FAR, NEAR, CORES, Y), ("x", "far", "near", "core", "y"))
    rows = ("x", "far", "near", "core")
    return jax.shard_map(
        per_device,
        mesh=fine,
        in_specs=(P(None, rows, "y"), P(None, rows, "y"), P("y", None)),
        out_specs=(P(None, rows, "y"), P("y", None)),
        check_vma=False,
    )
```
